32 devices in a mesh: frames: 8 (over y, x, core), pairs: 4 (over z).
Axes of the slice: x: 2, y: 2, z: 4, core: 2. Of those that a mesh axis runs over, the one named last changes fastest.
Arguments:
- coords: float32 [4096, 3, 384], P('frames'), may hold values from -3 to 3
- pair_first: int32 [256], P('pairs'), may hold values from 0 to 383
- pair_second: int32 [32768], P('pairs'), may hold values from 0 to 383
- enc_weight: bfloat16 [64, 32768], P(None, 'pairs'), may hold values from -0.03125 to 0.03125
- enc_bias: float32 [64], replicated, may hold values from -4 to 4
- dec_weight: bfloat16 [64, 32768], P(None, 'pairs'), may hold values from -0.75 to 0.75
- dec_bias: float32 [32768], P('pairs'), may hold values from -3 to 3
- lag_frames: int32 [1], replicated, may hold values from 256 to 512
Outputs:
- grad_enc: float32 [64, 32768], P(None, 'pairs')
- grad_dec: float32 [64, 32768], P(None, 'pairs')
The draws below stay inside these ranges and needn't reach their ends.
Inputs may be any that keep to these rules, and one draw needn't show every extreme that they name: Residue numbers; pair p joins residue pair_first[p // 128] with residue pair_second[p].
All inputs are finite; a program needn't handle non-finite values.
Results may differ from the reference program's by a relative error of at most 0.0003.
Values may be sent and summed in bfloat16 or wider, within the bound.
A program may use at most 192 MiB of HBM per device.

```python
import math
import jax
import jax.numpy as jnp
from jax import lax

FRAME_DEV = 512
LATENT = 64
RESIDUES = 384
FRAMES = 4096
PAIRS = 32768


def draw_coords(key, part):
    walk_key = jax.random.fold_in(key, 11)
    start_key = jax.random.fold_in(key, 12)
    noise_key = jax.random.fold_in(key, 13)
    reach = 0.45
    unit_step = reach / (math.sqrt(FRAME_DEV) * 37.0)
    half_span = int(1.75 / unit_step)
    coord_unit = 1.75 / half_span
    steps = jax.random.randint(walk_key, (FRAMES, 3, RESIDUES), -64, 65, dtype=jnp.int32)
    start = jax.random.randint(start_key, (1, 3, RESIDUES), 0, 2 * half_span, dtype=jnp.int32)
    walked = jnp.cumsum(steps, axis=0, dtype=jnp.int32) + start
    folded = walked % (2 * half_span)
    tent = half_span - jnp.abs(folded - half_span)
    centered = 2 * tent - half_span
    slow_part = centered.astype(jnp.float32) * coord_unit
    noise = jnp.clip(0.25 * jax.random.normal(noise_key, (FRAMES, 3, RESIDUES), jnp.float32), -1.0, 1.0)
    return (slow_part + noise).astype(jnp.float32)


def plant(values, key, smallest, high):
    place = [jax.random.randint(jax.random.fold_in(key, axis), (), 0, length) for axis, length in enumerate(values.shape)]
    longest = values.shape.index(max(values.shape))
    beside = place[:longest] + [(place[longest] + 1) % values.shape[longest]] + place[longest + 1:]
    return values.at[tuple(place)].set(smallest).at[tuple(beside)].set(high)


def levels(key, shape, shards, low, top_value):
    factor_of = 1.0
    for axis_at, shards_of in shards:
        draws = jax.random.uniform(jax.random.fold_in(jax.random.fold_in(key, 6), axis_at), (shards_of,), jnp.float32, low / len(shards), top_value / len(shards))
        factor_of = factor_of * jnp.repeat(jnp.exp(draws), shape[axis_at] // shards_of).reshape((-1,) + (1,) * (len(shape) - 1 - axis_at))
    return factor_of


def normal_values(rng, extent, scale, limit, cuts=(), kind=jnp.bfloat16):
    values = jax.random.normal(rng, extent, jnp.float32) * scale
    if len(cuts) > 0:
        values = levels(rng, extent, cuts, -0.22, 0.18) * values
    return jnp.clip(values, min=-limit, max=limit).astype(kind)


def setup_inputs(seed: int = 0) -> dict:
    streams_of = jax.random.split(jax.random.key(seed), 9)
    return {
        "coords": draw_coords(jax.random.fold_in(streams_of[8], 71), 0),
        "pair_first": plant(jax.random.randint(streams_of[1], (PAIRS // 128,), 0, RESIDUES), jax.random.fold_in(streams_of[1], 1), 0, RESIDUES - 1).astype(jnp.int32),
        "pair_second": plant(jax.random.randint(streams_of[2], (PAIRS,), 0, RESIDUES), jax.random.fold_in(streams_of[2], 1), 0, RESIDUES - 1).astype(jnp.int32),
        "enc_weight": normal_values(streams_of[3], (LATENT, PAIRS), PAIRS ** -0.5, 0.03125, ((1, 4),)),
        "enc_bias": normal_values(streams_of[4], (LATENT,), 1.0, 4.0, (), jnp.float32),
        "dec_weight": normal_values(streams_of[5], (LATENT, PAIRS), LATENT ** -0.5, 0.75, ((1, 4),)),
        "dec_bias": normal_values(streams_of[6], (PAIRS,), 0.5, 3.0, ((0, 4),), jnp.float32),
        "lag_frames": jax.random.randint(streams_of[7], (1,), FRAME_DEV // 2, FRAME_DEV + 1).astype(jnp.int32),
    }


cutoff_dist = 2.3
softness = 0.4

def contacts(frame_block, pair_first, pair_second):
    near = jnp.take(frame_block, pair_first, axis=2)
    far = jnp.take(frame_block, pair_second, axis=2)
    far = far.reshape(far.shape[0], 3, pair_first.shape[0], 128)
    offset = far - near[..., None]
    distance = jnp.sqrt(lax.optimization_barrier(jnp.sum(offset * offset, axis=1)))
    value = jax.nn.sigmoid((cutoff_dist - distance) / softness)
    return value.reshape(frame_block.shape[0], -1).astype(jnp.bfloat16)

def reference(coords, pair_first, pair_second, enc_weight, enc_bias, dec_weight, dec_bias, lag_frames):
    shift_now = lag_frames[0]
    padded = jnp.concatenate([coords, jnp.zeros((FRAME_DEV, 3, RESIDUES), coords.dtype)], axis=0)
    block_rows = min(256, FRAME_DEV)
    block_count = FRAMES // block_rows
    scale_factor = 1.0 / jnp.sqrt(jnp.float32(FRAMES) - shift_now.astype(jnp.float32))

    def step(totals, block_idx):
        grad_enc, grad_dec = totals
        begin_row = block_idx * block_rows
        own_coords = lax.dynamic_slice_in_dim(coords, begin_row, block_rows, 0)
        later_coords = lax.dynamic_slice_in_dim(padded, begin_row + shift_now, block_rows, 0)
        contact = contacts(own_coords, pair_first, pair_second)
        target = contacts(later_coords, pair_first, pair_second)
        hidden = lax.dot_general(enc_weight, contact, (((1,), (1,)), ((), ())), preferred_element_type=jnp.float32)
        latent = jnp.tanh(hidden + enc_bias[:, None])
        latent_bf = latent.astype(jnp.bfloat16)
        decoded = lax.dot_general(latent_bf, dec_weight, (((0,), (0,)), ((), ())), preferred_element_type=jnp.float32) + dec_bias[None, :]
        frame_ids = begin_row + jnp.arange(block_rows, dtype=jnp.int32)
        usable = frame_ids + shift_now < FRAMES
        err_bf = jnp.where(usable[:, None], (decoded - target.astype(jnp.float32)) * scale_factor, 0.0).astype(jnp.bfloat16)
        grad_dec = grad_dec + jnp.dot(latent_bf, err_bf, preferred_element_type=jnp.float32)
        backward = lax.dot_general(dec_weight, err_bf, (((1,), (1,)), ((), ())), preferred_element_type=jnp.float32)
        hidden_bf = (backward * (1.0 - latent * latent)).astype(jnp.bfloat16)
        grad_enc = grad_enc + jnp.dot(hidden_bf, contact, preferred_element_type=jnp.float32)
        return ((grad_enc, grad_dec), None)
    zeros = jnp.zeros((LATENT, PAIRS), jnp.float32)
    (grad_enc, grad_dec), unused = lax.scan(step, (zeros, zeros), jnp.arange(block_count, dtype=jnp.int32))
    return (grad_enc, grad_dec)
```

```python
from functools import partial

import jax
import jax.numpy as jnp
from jax import lax
from jax.experimental import pallas as pl
from jax.experimental.pallas import tpu as pltpu
from jax.sharding import PartitionSpec as P

cutoff_dist = 2.3
softness = 0.4
log2_e = 1.4426950408889634
pieces = 2
unit = 256


def split(value, count):
    parts = []
    rest = value
    for _ in range(count):
        part = rest.astype(jnp.bfloat16)
        parts.append(part)
        rest = rest - part.astype(jnp.float32)
    return parts


def contact_kernel(
    coords_ref, first_ref, second_ref, enc_ref, dec_ref, bias_ref,
    contact_ref, sums_ref, gram_ref, lean_ref, table, weights,
):
    step = pl.program_id(0)
    rows, residues = coords_ref.shape[1], coords_ref.shape[2]

    @pl.when(step == 0)
    def prepare():
        for axis in range(3):
            for i, part in enumerate(split(coords_ref[axis], pieces)):
                table[axis * rows:(axis + 1) * rows, i * residues:(i + 1) * residues] = part
        sums_ref[...] = jnp.zeros_like(sums_ref)
        gram_ref[...] = jnp.zeros_like(gram_ref)
        lean_ref[...] = jnp.zeros_like(lean_ref)

    width = first_ref.shape[1]
    latents = enc_ref.shape[0]
    weights[:latents, :] = enc_ref[...]
    weights[latents:, :] = dec_ref[...]
    gram_ref[...] += lax.dot_general(
        dec_ref[...], dec_ref[...], (((1,), (1,)), ((), ())), preferred_element_type=jnp.float32
    )
    lean = dec_ref[...].astype(jnp.float32) * bias_ref[...]
    for i in range(width // 128):
        lean_ref[...] += lean[:, i * 128:(i + 1) * 128]
    total = jnp.zeros(sums_ref.shape, jnp.float32)
    for i in range(width // unit):
        here = slice(i * unit, (i + 1) * unit)
        ids = lax.broadcasted_iota(jnp.int32, (residues, unit), 0)
        choice = (
            jnp.where(ids == second_ref[:, here], 1.0, 0.0) - jnp.where(ids == first_ref[:, here], 1.0, 0.0)
        ).astype(jnp.bfloat16)
        choice = jnp.concatenate([choice] * pieces, axis=0)
        square = jnp.zeros((rows, unit), jnp.float32)
        for axis in range(3):
            offset = jnp.dot(
                table[axis * rows:(axis + 1) * rows, :], choice, preferred_element_type=jnp.float32
            )
            square = square + offset * offset
        distance = square * lax.rsqrt(jnp.maximum(square, 1e-30))
        power = jnp.exp2(distance * (log2_e / softness) - cutoff_dist * log2_e / softness)
        contact = (1.0 / (1.0 + power)).astype(jnp.bfloat16)
        contact_ref[:, here] = contact
        total = total + lax.dot_general(
            contact, weights[:, here], (((1,), (1,)), ((), ())), preferred_element_type=jnp.float32
        )
    sums_ref[...] += total


def contacts(coords, first, second, enc_weight, dec_weight, dec_bias):
    rows, _, residues = coords.shape
    latents, pairs = enc_weight.shape
    width = min(512, pairs)
    row = pl.BlockSpec((1, width), lambda i: (0, i))
    block = pl.BlockSpec((latents, width), lambda i: (0, i))
    return pl.pallas_call(
        contact_kernel,
        grid=(pairs // width,),
        in_specs=[pl.BlockSpec((3, rows, residues), lambda i: (0, 0, 0)), row, row, block, block, row],
        out_specs=[
            pl.BlockSpec((rows, width), lambda i: (0, i)),
            pl.BlockSpec((rows, 2 * latents), lambda i: (0, 0)),
            pl.BlockSpec((latents, latents), lambda i: (0, 0)),
            pl.BlockSpec((latents, 128), lambda i: (0, 0)),
        ],
        out_shape=[
            jax.ShapeDtypeStruct((rows, pairs), jnp.bfloat16),
            jax.ShapeDtypeStruct((rows, 2 * latents), jnp.float32),
            jax.ShapeDtypeStruct((latents, latents), jnp.float32),
            jax.ShapeDtypeStruct((latents, 128), jnp.float32),
        ],
        scratch_shapes=[
            pltpu.VMEM((3 * rows, pieces * residues), jnp.bfloat16),
            pltpu.VMEM((2 * latents, width), jnp.bfloat16),
        ],
        compiler_params=pltpu.CompilerParams(vmem_limit_bytes=50 * 2**20),
        name="contacts",
    )(jnp.transpose(coords, (1, 0, 2)), first, second, enc_weight, dec_weight, dec_bias)


def grad_kernel(left_ref, mix_ref, scale_ref, contact_ref, dec_ref, bias_ref, enc_out, dec_out):
    latents = dec_ref.shape[0]
    product = jnp.dot(left_ref[...], contact_ref[...], preferred_element_type=jnp.float32)
    dec = dec_ref[...]
    own = jnp.dot(
        jnp.concatenate(split(mix_ref[...], 3), axis=1),
        jnp.concatenate([dec, dec, dec], axis=0),
        preferred_element_type=jnp.float32,
    )
    enc_out[...] = product[:latents]
    dec_out[...] = scale_ref[:, :1] * (own + scale_ref[:, 1:2] * bias_ref[...] - product[latents:])


def grads(left, mix, scale, contact, dec_weight, dec_bias):
    rows, pairs = contact.shape
    latents = dec_weight.shape[0]
    width = min(1024, pairs)
    whole = lambda a: pl.BlockSpec(a.shape, lambda i: (0, 0))
    out = pl.BlockSpec((latents, width), lambda i: (0, i))
    return pl.pallas_call(
        grad_kernel,
        grid=(pairs // width,),
        in_specs=[
            whole(left), whole(mix), whole(scale),
            pl.BlockSpec((rows, width), lambda i: (0, i)), out, pl.BlockSpec((1, width), lambda i: (0, i)),
        ],
        out_specs=[out, out],
        out_shape=[jax.ShapeDtypeStruct((latents, pairs), jnp.float32)] * 2,
        compiler_params=pltpu.CompilerParams(vmem_limit_bytes=40 * 2**20),
        name="grads",
    )(left, mix, scale, contact, dec_weight, dec_bias)


def middle(sums, gram, lean, own_rows, enc_bias, lag):
    rows, latents = sums.shape[0], gram.shape[0]
    devices = lax.axis_size("frames")
    total_frames = rows * devices
    latent = jnp.tanh(sums[:, :latents] + enc_bias[None, :])
    rounded = lax.reduce_precision(latent, 8, 7)
    latent_bf = rounded.astype(jnp.bfloat16)
    seen = sums[:, latents:]
    seen_next = lax.ppermute(seen, "frames", [(i, i - 1) for i in range(1, devices)])
    latent_prev = lax.ppermute(latent_bf, "frames", [(i, i + 1) for i in range(devices - 1)])
    seen_later = lax.dynamic_slice_in_dim(jnp.concatenate([seen, seen_next]), lag, rows, 0)
    latent_earlier = lax.dynamic_slice_in_dim(
        jnp.concatenate([latent_prev, latent_bf]), rows - lag, rows, 0
    )
    usable = (own_rows + lag < total_frames)[:, None]
    scale = 1.0 / jnp.sqrt(jnp.float32(total_frames) - lag.astype(jnp.float32))
    decoded = jnp.dot(rounded, gram, precision=lax.Precision.HIGHEST) + lean[None, :]
    backward = jnp.where(usable, (decoded - seen_later) * scale, 0.0)
    hidden_bf = (backward * (1.0 - latent * latent)).astype(jnp.bfloat16)
    used = jnp.where(usable, latent_bf, jnp.bfloat16(0))
    mix = lax.dot_general(used, used, (((0,), (0,)), ((), ())), preferred_element_type=jnp.float32)
    tilt = jnp.sum(used.astype(jnp.float32), axis=0)
    left = jnp.concatenate([hidden_bf, latent_earlier], axis=1).T
    scales = jnp.concatenate(
        [jnp.full((latents, 1), scale), tilt[:, None], jnp.zeros((latents, 126), jnp.float32)], axis=1
    )
    return left, mix, scales


def local(coords, pair_first, pair_second, enc_weight, enc_bias, dec_weight, dec_bias, lag_frames):
    rows = coords.shape[0]
    latents, pairs = enc_weight.shape
    first = jnp.broadcast_to(pair_first[:, None], (pairs // 128, 128)).reshape(1, pairs)
    bias = dec_bias.reshape(1, pairs)
    contact, sums, gram, lean = contacts(
        coords, first, pair_second.reshape(1, pairs), enc_weight, dec_weight, bias
    )
    small = jnp.concatenate([sums.reshape(-1), gram.reshape(-1), jnp.sum(lean, axis=1)])
    small = lax.psum(small, "pairs")
    sums = small[: sums.size].reshape(sums.shape)
    gram = small[sums.size : sums.size + gram.size].reshape(gram.shape)
    lean = small[sums.size + gram.size :]
    own_rows = lax.axis_index("frames") * rows + jnp.arange(rows, dtype=jnp.int32)
    left, mix, scales = middle(sums, gram, lean, own_rows, enc_bias, lag_frames[0])
    both = grads(left, mix, scales, contact, dec_weight, bias)
    return tuple(lax.psum(tuple(both), "frames"))


def solution(mesh):
    placed = (
        P("frames", None, None),
        P("pairs"),
        P("pairs"),
        P(None, "pairs"),
        P(),
        P(None, "pairs"),
        P("pairs"),
        P(),
    )
    return jax.shard_map(
        local,
        mesh=mesh,
        in_specs=placed,
        out_specs=(P(None, "pairs"), P(None, "pairs")),
        check_vma=False,
    )
```

```python
from functools import partial

import jax
import jax.numpy as jnp
from jax import lax
from jax.experimental import pallas as pl
from jax.experimental.pallas import tpu as pltpu
from jax.sharding import PartitionSpec as P

cutoff_dist = 2.3
softness = 0.4
log2_e = 1.4426950408889634
pieces = 2
unit = 256


def split(value, count):
    parts = []
    rest = value
    for _ in range(count):
        part = rest.astype(jnp.bfloat16)
        parts.append(part)
        rest = rest - part.astype(jnp.float32)
    return parts


def contact_kernel(
    coords_ref, first_ref, second_ref, enc_ref, dec_ref, contact_ref, sums_ref, table, weights
):
    step = pl.program_id(0)
    rows, residues = coords_ref.shape[1], coords_ref.shape[2]

    @pl.when(step == 0)
    def prepare():
        for axis in range(3):
            for i, part in enumerate(split(coords_ref[axis], pieces)):
                table[axis * rows:(axis + 1) * rows, i * residues:(i + 1) * residues] = part
        sums_ref[...] = jnp.zeros_like(sums_ref)

    width = first_ref.shape[1]
    latents = enc_ref.shape[0]
    weights[:latents, :] = enc_ref[...]
    weights[latents:, :] = dec_ref[...]
    total = jnp.zeros(sums_ref.shape, jnp.float32)
    for i in range(width // unit):
        here = slice(i * unit, (i + 1) * unit)
        ids = lax.broadcasted_iota(jnp.int32, (residues, unit), 0)
        choice = (
            jnp.where(ids == second_ref[:, here], 1.0, 0.0) - jnp.where(ids == first_ref[:, here], 1.0, 0.0)
        ).astype(jnp.bfloat16)
        choice = jnp.concatenate([choice] * pieces, axis=0)
        square = jnp.zeros((rows, unit), jnp.float32)
        for axis in range(3):
            offset = jnp.dot(
                table[axis * rows:(axis + 1) * rows, :], choice, preferred_element_type=jnp.float32
            )
            square = square + offset * offset
        distance = square * lax.rsqrt(jnp.maximum(square, 1e-30))
        power = jnp.exp2(distance * (log2_e / softness) - cutoff_dist * log2_e / softness)
        contact = (1.0 / (1.0 + power)).astype(jnp.bfloat16)
        contact_ref[:, here] = contact
        total = total + lax.dot_general(
            contact, weights[:, here], (((1,), (1,)), ((), ())), preferred_element_type=jnp.float32
        )
    sums_ref[...] += total


def contacts(coords, first, second, enc_weight, dec_weight):
    rows, _, residues = coords.shape
    latents, pairs = enc_weight.shape
    width = min(512, pairs)
    row = pl.BlockSpec((1, width), lambda i: (0, i))
    block = pl.BlockSpec((latents, width), lambda i: (0, i))
    return pl.pallas_call(
        contact_kernel,
        grid=(pairs // width,),
        in_specs=[pl.BlockSpec((3, rows, residues), lambda i: (0, 0, 0)), row, row, block, block],
        out_specs=[
            pl.BlockSpec((rows, width), lambda i: (0, i)),
            pl.BlockSpec((rows, 2 * latents), lambda i: (0, 0)),
        ],
        out_shape=[
            jax.ShapeDtypeStruct((rows, pairs), jnp.bfloat16),
            jax.ShapeDtypeStruct((rows, 2 * latents), jnp.float32),
        ],
        scratch_shapes=[
            pltpu.VMEM((3 * rows, pieces * residues), jnp.bfloat16),
            pltpu.VMEM((2 * latents, width), jnp.bfloat16),
        ],
        compiler_params=pltpu.CompilerParams(vmem_limit_bytes=50 * 2**20),
        cost_estimate=pl.CostEstimate(
            flops=2 * 3 * rows * pieces * residues * pairs,
            bytes_accessed=4 * rows * pairs,
            transcendentals=3 * rows * pairs,
        ),
        name="contacts",
    )(jnp.transpose(coords, (1, 0, 2)), first, second, enc_weight, dec_weight)


def tail_kernel(
    chunks, lag_ref, scale_ref, enc_bias_ref, sums_ref, gram_ref, lean_ref, dec_ref, bias_ref, contact_any,
    out_ref, contact_ref, zrecv, whole, seen_send, seen_recv, lat_send, lat_recv, left_ref, partial_sum, arrived,
    contact_sem, z_send, z_recv, side_send, side_recv, half_send, half_recv, full_send, full_recv,
):
    frames, pairs = lax.axis_size("frames"), lax.axis_size("pairs")
    me, depth = lax.axis_index("frames"), lax.axis_index("pairs")
    bits = frames.bit_length() - 1
    rows, latents = sums_ref.shape[0], dec_ref.shape[0]
    part = rows // pairs
    width = dec_ref.shape[1] // chunks
    shard = width // frames
    half = rows // 2

    def partner(bit):
        return me + (1 << bit) - 2 * (1 << bit) * (lax.div(me, 1 << bit) % 2)

    def bit_of(bit):
        return lax.div(me, 1 << bit) % 2

    following, previous = lax.rem(me + 1, frames), lax.rem(me + frames - 1, frames)

    load = pltpu.make_async_copy(contact_any, contact_ref, contact_sem)
    load.start()
    barrier = pltpu.get_barrier_semaphore()
    for step in range(1, pairs):
        pl.semaphore_signal(
            barrier, inc=1, device_id={"pairs": lax.rem(depth + step, pairs)}, device_id_type=pl.DeviceIdType.MESH
        )
    for other in [following, previous] + [partner(b) for b in range(bits)]:
        pl.semaphore_signal(barrier, inc=1, device_id={"frames": other}, device_id_type=pl.DeviceIdType.MESH)
    pl.semaphore_wait(barrier, pairs - 1 + 2 + bits)

    def part_rows(index):
        return pl.ds(pl.multiple_of(index * part, part), part)

    scatter = []
    for step in range(1, pairs):
        other = lax.rem(depth + step, pairs)
        copy = pltpu.make_async_remote_copy(
            src_ref=sums_ref.at[part_rows(other)],
            dst_ref=zrecv.at[step - 1],
            send_sem=z_send.at[0, step - 1],
            recv_sem=z_recv.at[0, step - 1],
            device_id={"pairs": other},
            device_id_type=pl.DeviceIdType.MESH,
        )
        copy.start()
        scatter.append(copy)
    total = sums_ref[part_rows(depth), :]
    for step in range(1, pairs):
        scatter[step - 1].wait_recv()
        total = total + zrecv[step - 1]
    whole[part_rows(depth), :] = total
    gather = []
    for step in range(1, pairs):
        copy = pltpu.make_async_remote_copy(
            src_ref=whole.at[part_rows(depth)],
            dst_ref=whole.at[part_rows(depth)],
            send_sem=z_send.at[1, step - 1],
            recv_sem=z_recv.at[1, step - 1],
            device_id={"pairs": lax.rem(depth + step, pairs)},
            device_id_type=pl.DeviceIdType.MESH,
        )
        copy.start()
        gather.append(copy)
    for copy in gather:
        copy.wait_recv()

    latent = jnp.tanh(whole[:, :latents] + enc_bias_ref[...])
    latent_bf = latent.astype(jnp.bfloat16)
    seen = whole[:, latents:]
    seen_send[...] = jnp.concatenate([seen[:half], seen[half:]], axis=1)
    lat_send[...] = jnp.concatenate([latent_bf[:half], latent_bf[half:]], axis=1)
    sides = []
    for i, (source, target, other) in enumerate(
        [(seen_send, seen_recv, previous), (lat_send, lat_recv, following)]
    ):
        copy = pltpu.make_async_remote_copy(
            src_ref=source,
            dst_ref=target,
            send_sem=side_send.at[i],
            recv_sem=side_recv.at[i],
            device_id={"frames": other},
            device_id_type=pl.DeviceIdType.MESH,
        )
        copy.start()
        sides.append(copy)

    lag = lag_ref[...]
    scale = scale_ref[...]
    frame = lax.broadcasted_iota(jnp.int32, (rows, 1), 0)
    usable = me * rows + frame + lag < rows * frames
    used = jnp.where(usable, latent_bf.astype(jnp.float32), 0.0).astype(jnp.bfloat16)
    mix = lax.dot_general(used, used, (((0,), (0,)), ((), ())), preferred_element_type=jnp.float32)
    tilt = lax.dot_general(
        used, jnp.ones((rows, 128), jnp.bfloat16), (((0,), (0,)), ((), ())), preferred_element_type=jnp.float32
    )[:, :1]
    mix_parts = jnp.concatenate(split(mix, 3), axis=1)
    decoded = lean_ref[...]
    for piece in split(gram_ref[...], 3):
        decoded = decoded + jnp.dot(latent_bf, piece, preferred_element_type=jnp.float32)
    for copy in sides:
        copy.wait_recv()
    seen_all = jnp.concatenate([seen, seen_recv[:, :latents], seen_recv[:, latents:]], axis=0)
    latent_all = jnp.concatenate([lat_recv[:, :latents], lat_recv[:, latents:], latent_bf], axis=0)
    place = lax.broadcasted_iota(jnp.int32, (rows, 2 * rows), 1)
    pick_later = jnp.where(place == frame + lag, 1.0, 0.0).astype(jnp.bfloat16)
    pick_earlier = jnp.where(place == frame + rows - lag, 1.0, 0.0).astype(jnp.bfloat16)
    later = jnp.zeros((rows, latents), jnp.float32)
    for piece in split(seen_all, 3):
        later = later + jnp.dot(pick_later, piece, preferred_element_type=jnp.float32)
    earlier = jnp.dot(pick_earlier, latent_all, preferred_element_type=jnp.float32)
    earlier = jnp.where(me * rows + frame >= lag, earlier, 0.0)
    backward = jnp.where(usable, (decoded - later) * scale, 0.0)
    hidden = backward * (1.0 - latent * latent)
    left_ref[...] = jnp.transpose(jnp.concatenate([hidden, earlier], axis=1)).astype(jnp.bfloat16)
    load.wait()

    def order(color):
        turn = color % max(bits - 1, 1)
        later_bits = list(range(1, bits))
        return [0] + later_bits[turn:] + later_bits[:turn]

    def begin_of(sequence, count):
        begin = 0
        for k in range(count):
            begin = begin + bit_of(sequence[k]) * (frames >> (k + 1))
        return begin

    def halving(chunk, sequence, k):
        size = frames >> (k + 1)
        begin = begin_of(sequence, k) + (1 - bit_of(sequence[k])) * size
        return pltpu.make_async_remote_copy(
            src_ref=partial_sum.at[chunk, pl.ds(begin, size)],
            dst_ref=arrived.at[chunk, pl.ds(frames - 2 * size, size)],
            send_sem=half_send.at[chunk, k],
            recv_sem=half_recv.at[chunk, k],
            device_id={"frames": partner(sequence[k])},
            device_id_type=pl.DeviceIdType.MESH,
        )

    def doubling(chunk, sequence, k):
        size = frames >> (k + 1)
        columns = pl.ds(
            pl.multiple_of(chunk * width + begin_of(sequence, k + 1) * shard, shard), size * shard
        )
        return pltpu.make_async_remote_copy(
            src_ref=out_ref.at[:, columns],
            dst_ref=out_ref.at[:, columns],
            send_sem=full_send.at[chunk, k],
            recv_sem=full_recv.at[chunk, k],
            device_id={"frames": partner(sequence[k])},
            device_id_type=pl.DeviceIdType.MESH,
        )

    def each_chunk(body):
        def pair(index, carry):
            for color in range(2):
                body(index * 2 + color, order(color))
            return carry

        lax.fori_loop(0, chunks // 2, pair, 0)

    def multiply(chunk, sequence):
        columns = pl.ds(pl.multiple_of(chunk * width, width), width)
        product = jnp.dot(left_ref[...], contact_ref[:, columns], preferred_element_type=jnp.float32)
        dec = dec_ref[:, columns]
        own = jnp.dot(mix_parts, jnp.concatenate([dec, dec, dec], axis=0), preferred_element_type=jnp.float32)
        decode = scale * (own + tilt * bias_ref[:, columns] - product[latents:])
        for i in range(frames):
            here = slice(i * shard, (i + 1) * shard)
            partial_sum[chunk, i, :latents] = product[:latents, here]
            partial_sum[chunk, i, latents:] = decode[:, here]
        halving(chunk, sequence, 0).start()

    each_chunk(multiply)
    for k in range(bits):
        def reduce(chunk, sequence, k=k):
            halving(chunk, sequence, k).wait_recv()
            size = frames >> (k + 1)
            begin = begin_of(sequence, k + 1)
            added = partial_sum[chunk, pl.ds(begin, size)] + arrived[chunk, pl.ds(frames - 2 * size, size)]
            if k < bits - 1:
                partial_sum[chunk, pl.ds(begin, size)] = added
                halving(chunk, sequence, k + 1).start()
            else:
                columns = pl.ds(pl.multiple_of(chunk * width + begin * shard, shard), shard)
                out_ref[:, columns] = added[0]
                doubling(chunk, sequence, k).start()

        each_chunk(reduce)
    for k in reversed(range(bits)):
        def spread(chunk, sequence, k=k):
            doubling(chunk, sequence, k).wait_recv()
            if k > 0:
                doubling(chunk, sequence, k - 1).start()

        each_chunk(spread)

    def finish(chunk, sequence):
        for k in range(bits):
            halving(chunk, sequence, k).wait_send()
            doubling(chunk, sequence, k).wait_send()

    each_chunk(finish)
    for copy in scatter + gather + sides:
        copy.wait_send()


def tail(lag, scale, enc_bias, sums, gram, lean, dec_weight, dec_bias, contact):
    rows, pairs = contact.shape
    latents = dec_weight.shape[0]
    frames, depth = lax.axis_size("frames"), lax.axis_size("pairs")
    bits = frames.bit_length() - 1
    chunks = 2 * max(1, min(4, pairs // (2 * frames * 128)))
    shard = pairs // chunks // frames
    vmem = pl.BlockSpec(memory_space=pltpu.VMEM)
    dma = pltpu.SemaphoreType.DMA
    return pl.pallas_call(
        partial(tail_kernel, chunks),
        in_specs=[vmem] * 8 + [pl.BlockSpec(memory_space=pl.ANY)],
        out_specs=vmem,
        out_shape=jax.ShapeDtypeStruct((2 * latents, pairs), jnp.float32),
        scratch_shapes=[
            pltpu.VMEM((rows, pairs), jnp.bfloat16),
            pltpu.VMEM((depth - 1, rows // depth, 2 * latents), jnp.float32),
            pltpu.VMEM((rows, 2 * latents), jnp.float32),
            pltpu.VMEM((rows // 2, 2 * latents), jnp.float32),
            pltpu.VMEM((rows // 2, 2 * latents), jnp.float32),
            pltpu.VMEM((rows // 2, 2 * latents), jnp.bfloat16),
            pltpu.VMEM((rows // 2, 2 * latents), jnp.bfloat16),
            pltpu.VMEM((2 * latents, rows), jnp.bfloat16),
            pltpu.VMEM((chunks, frames, 2 * latents, shard), jnp.float32),
            pltpu.VMEM((chunks, frames - 1, 2 * latents, shard), jnp.float32),
            dma,
            dma((2, depth - 1)),
            dma((2, depth - 1)),
            dma((2,)),
            dma((2,)),
            dma((chunks, bits)),
            dma((chunks, bits)),
            dma((chunks, bits)),
            dma((chunks, bits)),
        ],
        compiler_params=pltpu.CompilerParams(
            vmem_limit_bytes=50 * 2**20, collective_id=0, has_side_effects=True
        ),
        name="tail",
    )(lag, scale, enc_bias, sums, gram, lean, dec_weight, dec_bias, contact)


def local(coords, pair_first, pair_second, enc_weight, enc_bias, dec_weight, dec_bias, lag_frames):
    rows = coords.shape[0]
    latents, pairs = enc_weight.shape
    total_frames = rows * lax.axis_size("frames")
    first = jnp.broadcast_to(pair_first[:, None], (pairs // 128, 128)).reshape(1, pairs)
    bias = dec_bias.reshape(1, pairs)
    gram = lax.dot_general(
        dec_weight, dec_weight, (((1,), (1,)), ((), ())), preferred_element_type=jnp.float32
    )
    lean = jnp.sum(dec_weight.astype(jnp.float32) * bias, axis=1)
    small = lax.psum(jnp.concatenate([gram, lean[None, :]]), "pairs")
    contact, sums = contacts(coords, first, pair_second.reshape(1, pairs), enc_weight, dec_weight)
    scale = 1.0 / jnp.sqrt(jnp.float32(total_frames) - lag_frames.astype(jnp.float32))
    both = tail(
        lag_frames.reshape(1, 1), scale.reshape(1, 1), enc_bias.reshape(1, latents), sums,
        small[:latents], small[latents:], dec_weight, bias, contact,
    )
    return both[:latents], both[latents:]


def solution(mesh):
    placed = (
        P("frames", None, None),
        P("pairs"),
        P("pairs"),
        P(None, "pairs"),
        P(),
        P(None, "pairs"),
        P("pairs"),
        P(),
    )
    return jax.shard_map(
        local,
        mesh=mesh,
        in_specs=placed,
        out_specs=(P(None, "pairs"), P(None, "pairs")),
        check_vma=False,
    )
```

```python
from functools import partial

import jax
import jax.numpy as jnp
from jax import lax
from jax.experimental import pallas as pl
from jax.experimental.pallas import tpu as pltpu
from jax.sharding import PartitionSpec as P

cutoff_dist = 2.3
softness = 0.4
log2_e = 1.4426950408889634
pieces = 2
unit = 256


def split(value, count):
    parts = []
    rest = value
    for _ in range(count):
        part = rest.astype(jnp.bfloat16)
        parts.append(part)
        rest = rest - part.astype(jnp.float32)
    return parts


def contact_kernel(
    coords_ref, first_ref, second_ref, enc_ref, dec_ref, bias_ref, contact_ref, out_ref, table, weights,
    sums_ref, gram_ref, lean_ref,

):
    step = pl.program_id(0)
    rows, residues = coords_ref.shape[1], coords_ref.shape[2]

    @pl.when(step == 0)
    def prepare():
        for axis in range(3):
            for i, part in enumerate(split(coords_ref[axis], pieces)):
                table[axis * rows:(axis + 1) * rows, i * residues:(i + 1) * residues] = part
        sums_ref[...] = jnp.zeros_like(sums_ref)
        gram_ref[...] = jnp.zeros_like(gram_ref)
        lean_ref[...] = jnp.zeros_like(lean_ref)

    width = first_ref.shape[1]
    latents = enc_ref.shape[0]
    weights[:latents, :] = enc_ref[...]
    weights[latents:, :] = dec_ref[...]
    gram_ref[...] += lax.dot_general(
        dec_ref[...], dec_ref[...], (((1,), (1,)), ((), ())), preferred_element_type=jnp.float32
    )
    lean = dec_ref[...].astype(jnp.float32) * bias_ref[...]
    for i in range(width // 128):
        lean_ref[...] += lean[:, i * 128:(i + 1) * 128]
    total = jnp.zeros(sums_ref.shape, jnp.float32)
    for i in range(width // unit):
        here = slice(i * unit, (i + 1) * unit)
        ids = lax.broadcasted_iota(jnp.int32, (residues, unit), 0)
        choice = (
            jnp.where(ids == second_ref[:, here], 1.0, 0.0) - jnp.where(ids == first_ref[:, here], 1.0, 0.0)
        ).astype(jnp.bfloat16)
        choice = jnp.concatenate([choice] * pieces, axis=0)
        square = jnp.zeros((rows, unit), jnp.float32)
        for axis in range(3):
            offset = jnp.dot(
                table[axis * rows:(axis + 1) * rows, :], choice, preferred_element_type=jnp.float32
            )
            square = square + offset * offset
        distance = square * lax.rsqrt(jnp.maximum(square, 1e-30))
        power = jnp.exp2(distance * (log2_e / softness) - cutoff_dist * log2_e / softness)
        contact = (1.0 / (1.0 + power)).astype(jnp.bfloat16)
        contact_ref[:, here] = contact
        total = total + lax.dot_general(
            contact, weights[:, here], (((1,), (1,)), ((), ())), preferred_element_type=jnp.float32
        )
    sums_ref[...] += total

    @pl.when(step == pl.num_programs(0) - 1)
    def finish():
        parts = out_ref.shape[0]
        part, few = rows // parts, latents // parts
        lean = jnp.broadcast_to(jnp.sum(lean_ref[...], axis=1, keepdims=True), (latents, latents))
        small = jnp.concatenate([gram_ref[...], lean], axis=1)
        for i in range(parts):
            out_ref[i, :part] = sums_ref[i * part:(i + 1) * part, :]
            out_ref[i, part:] = small[i * few:(i + 1) * few]


def contacts(coords, first, second, enc_weight, dec_weight, dec_bias):
    rows, _, residues = coords.shape
    latents, pairs = enc_weight.shape
    width = min(512, pairs)
    parts = lax.axis_size("pairs")
    sent = (parts, (rows + latents) // parts, 2 * latents)
    row = pl.BlockSpec((1, width), lambda i: (0, i))
    block = pl.BlockSpec((latents, width), lambda i: (0, i))
    return pl.pallas_call(
        contact_kernel,
        grid=(pairs // width,),
        in_specs=[pl.BlockSpec((3, rows, residues), lambda i: (0, 0, 0)), row, row, block, block, row],
        out_specs=[
            pl.BlockSpec((rows, width), lambda i: (0, i)),
            pl.BlockSpec(sent, lambda i: (0, 0, 0)),
        ],
        out_shape=[
            jax.ShapeDtypeStruct((rows, pairs), jnp.bfloat16),
            jax.ShapeDtypeStruct(sent, jnp.float32),
        ],
        scratch_shapes=[
            pltpu.VMEM((3 * rows, pieces * residues), jnp.bfloat16),
            pltpu.VMEM((2 * latents, width), jnp.bfloat16),
            pltpu.VMEM((rows, 2 * latents), jnp.float32),
            pltpu.VMEM((latents, latents), jnp.float32),
            pltpu.VMEM((latents, 128), jnp.float32),
        ],
        compiler_params=pltpu.CompilerParams(vmem_limit_bytes=50 * 2**20),
        cost_estimate=pl.CostEstimate(
            flops=2 * 3 * rows * pieces * residues * pairs,
            bytes_accessed=4 * rows * pairs,
            transcendentals=3 * rows * pairs,
        ),
        name="contacts",
    )(jnp.transpose(coords, (1, 0, 2)), first, second, enc_weight, dec_weight, dec_bias)


def tail_kernel(
    chunks, lag_ref, scale_ref, enc_bias_ref, sums_ref, dec_ref, bias_ref, contact_any,
    out_ref, contact_ref, zrecv, whole, seen_send, seen_recv, lat_send, lat_recv, left_ref, partial_sum, arrived,
    contact_sem, z_send, z_recv, side_send, side_recv, half_send, half_recv, full_send, full_recv,
):
    frames, pairs = lax.axis_size("frames"), lax.axis_size("pairs")
    me, depth = lax.axis_index("frames"), lax.axis_index("pairs")
    bits = frames.bit_length() - 1
    rows, latents = contact_any.shape[0], dec_ref.shape[0]
    part = rows // pairs
    width = dec_ref.shape[1] // chunks
    shard = width // frames
    half = rows // 2

    def partner(bit):
        return me + (1 << bit) - 2 * (1 << bit) * (lax.div(me, 1 << bit) % 2)

    def bit_of(bit):
        return lax.div(me, 1 << bit) % 2

    following, previous = lax.rem(me + 1, frames), lax.rem(me + frames - 1, frames)

    load = pltpu.make_async_copy(contact_any, contact_ref, contact_sem)
    load.start()
    barrier = pltpu.get_barrier_semaphore()
    for step in range(1, pairs):
        pl.semaphore_signal(
            barrier, inc=1, device_id={"pairs": lax.rem(depth + step, pairs)}, device_id_type=pl.DeviceIdType.MESH
        )
    for other in [following, previous] + [partner(b) for b in range(bits)]:
        pl.semaphore_signal(barrier, inc=1, device_id={"frames": other}, device_id_type=pl.DeviceIdType.MESH)
    pl.semaphore_wait(barrier, pairs - 1 + 2 + bits)

    scatter = []
    for step in range(1, pairs):
        other = lax.rem(depth + step, pairs)
        copy = pltpu.make_async_remote_copy(
            src_ref=sums_ref.at[other],
            dst_ref=zrecv.at[step - 1],
            send_sem=z_send.at[0, step - 1],
            recv_sem=z_recv.at[0, step - 1],
            device_id={"pairs": other},
            device_id_type=pl.DeviceIdType.MESH,
        )
        copy.start()
        scatter.append(copy)
    total = sums_ref[depth]
    for step in range(1, pairs):
        scatter[step - 1].wait_recv()
        total = total + zrecv[step - 1]
    whole[depth] = total
    gather = []
    for step in range(1, pairs):
        copy = pltpu.make_async_remote_copy(
            src_ref=whole.at[depth],
            dst_ref=whole.at[depth],
            send_sem=z_send.at[1, step - 1],
            recv_sem=z_recv.at[1, step - 1],
            device_id={"pairs": lax.rem(depth + step, pairs)},
            device_id_type=pl.DeviceIdType.MESH,
        )
        copy.start()
        gather.append(copy)
    for copy in gather:
        copy.wait_recv()

    sums = jnp.concatenate([whole[i, :part] for i in range(pairs)], axis=0)
    small = jnp.concatenate([whole[i, part:] for i in range(pairs)], axis=0)
    gram = small[:, :latents]
    lean = jnp.transpose(small)[latents:latents + 1, :]
    latent = jnp.tanh(sums[:, :latents] + enc_bias_ref[...])
    latent_bf = latent.astype(jnp.bfloat16)
    seen = sums[:, latents:]
    seen_send[...] = jnp.concatenate([seen[:half], seen[half:]], axis=1)
    lat_send[...] = jnp.concatenate([latent_bf[:half], latent_bf[half:]], axis=1)
    sides = []
    for i, (source, target, other) in enumerate(
        [(seen_send, seen_recv, previous), (lat_send, lat_recv, following)]
    ):
        copy = pltpu.make_async_remote_copy(
            src_ref=source,
            dst_ref=target,
            send_sem=side_send.at[i],
            recv_sem=side_recv.at[i],
            device_id={"frames": other},
            device_id_type=pl.DeviceIdType.MESH,
        )
        copy.start()
        sides.append(copy)

    lag = lag_ref[...]
    scale = scale_ref[...]
    frame = lax.broadcasted_iota(jnp.int32, (rows, 1), 0)
    usable = me * rows + frame + lag < rows * frames
    used = jnp.where(usable, latent_bf.astype(jnp.float32), 0.0).astype(jnp.bfloat16)
    mix = lax.dot_general(used, used, (((0,), (0,)), ((), ())), preferred_element_type=jnp.float32)
    tilt = lax.dot_general(
        used, jnp.ones((rows, 128), jnp.bfloat16), (((0,), (0,)), ((), ())), preferred_element_type=jnp.float32
    )[:, :1]
    mix_parts = jnp.concatenate(split(mix, 3), axis=1)
    decoded = lean
    for piece in split(gram, 3):
        decoded = decoded + jnp.dot(latent_bf, piece, preferred_element_type=jnp.float32)
    for copy in sides:
        copy.wait_recv()
    seen_all = jnp.concatenate([seen, seen_recv[:, :latents], seen_recv[:, latents:]], axis=0)
    latent_all = jnp.concatenate([lat_recv[:, :latents], lat_recv[:, latents:], latent_bf], axis=0)
    place = lax.broadcasted_iota(jnp.int32, (rows, 2 * rows), 1)
    pick_later = jnp.where(place == frame + lag, 1.0, 0.0).astype(jnp.bfloat16)
    pick_earlier = jnp.where(place == frame + rows - lag, 1.0, 0.0).astype(jnp.bfloat16)
    later = jnp.zeros((rows, latents), jnp.float32)
    for piece in split(seen_all, 3):
        later = later + jnp.dot(pick_later, piece, preferred_element_type=jnp.float32)
    earlier = jnp.dot(pick_earlier, latent_all, preferred_element_type=jnp.float32)
    earlier = jnp.where(me * rows + frame >= lag, earlier, 0.0)
    backward = jnp.where(usable, (decoded - later) * scale, 0.0)
    hidden = backward * (1.0 - latent * latent)
    left_ref[...] = jnp.transpose(jnp.concatenate([hidden, earlier], axis=1)).astype(jnp.bfloat16)
    load.wait()

    def order(color):
        turn = color % max(bits - 1, 1)
        later_bits = list(range(1, bits))
        return [0] + later_bits[turn:] + later_bits[:turn]

    def begin_of(sequence, count):
        begin = 0
        for k in range(count):
            begin = begin + bit_of(sequence[k]) * (frames >> (k + 1))
        return begin

    def halving(chunk, sequence, k):
        size = frames >> (k + 1)
        begin = begin_of(sequence, k) + (1 - bit_of(sequence[k])) * size
        return pltpu.make_async_remote_copy(
            src_ref=partial_sum.at[chunk, pl.ds(begin, size)],
            dst_ref=arrived.at[chunk, pl.ds(frames - 2 * size, size)],
            send_sem=half_send.at[chunk, k],
            recv_sem=half_recv.at[chunk, k],
            device_id={"frames": partner(sequence[k])},
            device_id_type=pl.DeviceIdType.MESH,
        )

    def doubling(chunk, sequence, k):
        size = frames >> (k + 1)
        columns = pl.ds(
            pl.multiple_of(chunk * width + begin_of(sequence, k + 1) * shard, shard), size * shard
        )
        return pltpu.make_async_remote_copy(
            src_ref=out_ref.at[:, columns],
            dst_ref=out_ref.at[:, columns],
            send_sem=full_send.at[chunk, k],
            recv_sem=full_recv.at[chunk, k],
            device_id={"frames": partner(sequence[k])},
            device_id_type=pl.DeviceIdType.MESH,
        )

    def each_chunk(body):
        def pair(index, carry):
            for color in range(2):
                body(index * 2 + color, order(color))
            return carry

        lax.fori_loop(0, chunks // 2, pair, 0)

    def multiply(chunk, sequence):
        columns = pl.ds(pl.multiple_of(chunk * width, width), width)
        product = jnp.dot(left_ref[...], contact_ref[:, columns], preferred_element_type=jnp.float32)
        dec = dec_ref[:, columns]
        own = jnp.dot(mix_parts, jnp.concatenate([dec, dec, dec], axis=0), preferred_element_type=jnp.float32)
        decode = scale * (own + tilt * bias_ref[:, columns] - product[latents:])
        for i in range(frames):
            here = slice(i * shard, (i + 1) * shard)
            partial_sum[chunk, i, :latents] = product[:latents, here]
            partial_sum[chunk, i, latents:] = decode[:, here]
        halving(chunk, sequence, 0).start()

    each_chunk(multiply)
    for k in range(bits):
        def reduce(chunk, sequence, k=k):
            halving(chunk, sequence, k).wait_recv()
            size = frames >> (k + 1)
            begin = begin_of(sequence, k + 1)
            added = partial_sum[chunk, pl.ds(begin, size)] + arrived[chunk, pl.ds(frames - 2 * size, size)]
            if k < bits - 1:
                partial_sum[chunk, pl.ds(begin, size)] = added
                halving(chunk, sequence, k + 1).start()
            else:
                columns = pl.ds(pl.multiple_of(chunk * width + begin * shard, shard), shard)
                out_ref[:, columns] = added[0]
                doubling(chunk, sequence, k).start()

        each_chunk(reduce)
    for k in reversed(range(bits)):
        def spread(chunk, sequence, k=k):
            doubling(chunk, sequence, k).wait_recv()
            if k > 0:
                doubling(chunk, sequence, k - 1).start()

        each_chunk(spread)

    def finish(chunk, sequence):
        for k in range(bits):
            halving(chunk, sequence, k).wait_send()
            doubling(chunk, sequence, k).wait_send()

    each_chunk(finish)
    for copy in scatter + gather + sides:
        copy.wait_send()


def tail(lag, scale, enc_bias, sums, dec_weight, dec_bias, contact):
    rows, pairs = contact.shape
    latents = dec_weight.shape[0]
    frames, depth = lax.axis_size("frames"), lax.axis_size("pairs")
    bits = frames.bit_length() - 1
    chunks = 2 * max(1, min(4, pairs // (2 * frames * 128)))
    shard = pairs // chunks // frames
    vmem = pl.BlockSpec(memory_space=pltpu.VMEM)
    dma = pltpu.SemaphoreType.DMA
    return pl.pallas_call(
        partial(tail_kernel, chunks),
        in_specs=[vmem] * 6 + [pl.BlockSpec(memory_space=pl.ANY)],
        out_specs=vmem,
        out_shape=jax.ShapeDtypeStruct((2 * latents, pairs), jnp.float32),
        scratch_shapes=[
            pltpu.VMEM((rows, pairs), jnp.bfloat16),
            pltpu.VMEM((depth - 1, *sums.shape[1:]), jnp.float32),
            pltpu.VMEM(sums.shape, jnp.float32),
            pltpu.VMEM((rows // 2, 2 * latents), jnp.float32),
            pltpu.VMEM((rows // 2, 2 * latents), jnp.float32),
            pltpu.VMEM((rows // 2, 2 * latents), jnp.bfloat16),
            pltpu.VMEM((rows // 2, 2 * latents), jnp.bfloat16),
            pltpu.VMEM((2 * latents, rows), jnp.bfloat16),
            pltpu.VMEM((chunks, frames, 2 * latents, shard), jnp.float32),
            pltpu.VMEM((chunks, frames - 1, 2 * latents, shard), jnp.float32),
            dma,
            dma((2, depth - 1)),
            dma((2, depth - 1)),
            dma((2,)),
            dma((2,)),
            dma((chunks, bits)),
            dma((chunks, bits)),
            dma((chunks, bits)),
            dma((chunks, bits)),
        ],
        compiler_params=pltpu.CompilerParams(
            vmem_limit_bytes=50 * 2**20, collective_id=0, has_side_effects=True
        ),
        name="tail",
    )(lag, scale, enc_bias, sums, dec_weight, dec_bias, contact)


def local(coords, pair_first, pair_second, enc_weight, enc_bias, dec_weight, dec_bias, lag_frames):
    rows = coords.shape[0]
    latents, pairs = enc_weight.shape
    total_frames = rows * lax.axis_size("frames")
    first = jnp.broadcast_to(pair_first[:, None], (pairs // 128, 128)).reshape(1, pairs)
    bias = dec_bias.reshape(1, pairs)
    contact, sums = contacts(coords, first, pair_second.reshape(1, pairs), enc_weight, dec_weight, bias)
    scale = 1.0 / jnp.sqrt(jnp.float32(total_frames) - lag_frames.astype(jnp.float32))
    both = tail(
        lag_frames.reshape(1, 1), scale.reshape(1, 1), enc_bias.reshape(1, latents), sums,
        dec_weight, bias, contact,
    )
    return both[:latents], both[latents:]


def solution(mesh):
    placed = (
        P("frames", None, None),
        P("pairs"),
        P("pairs"),
        P(None, "pairs"),
        P(),
        P(None, "pairs"),
        P("pairs"),
        P(),
    )
    return jax.shard_map(
        local,
        mesh=mesh,
        in_specs=placed,
        out_specs=(P(None, "pairs"), P(None, "pairs")),
        check_vma=False,
    )
```

```python
from functools import partial

import jax
import jax.numpy as jnp
from jax import lax
from jax.experimental import pallas as pl
from jax.experimental.pallas import tpu as pltpu
from jax.sharding import PartitionSpec as P

cutoff_dist = 2.3
softness = 0.4
log2_e = 1.4426950408889634
pieces = 2
unit = 256


def split(value, count):
    parts = []
    rest = value
    for _ in range(count):
        part = rest.astype(jnp.bfloat16)
        parts.append(part)
        rest = rest - part.astype(jnp.float32)
    return parts


def contact_kernel(
    coords_ref, first_ref, second_ref, enc_ref, dec_ref, bias_ref, contact_ref, out_ref, table, weights,
    sums_ref, gram_ref, lean_ref,

):
    step = pl.program_id(0)
    rows, residues = coords_ref.shape[1], coords_ref.shape[2]

    @pl.when(step == 0)
    def prepare():
        for axis in range(3):
            for i, part in enumerate(split(coords_ref[axis], pieces)):
                table[axis * rows:(axis + 1) * rows, i * residues:(i + 1) * residues] = part
        sums_ref[...] = jnp.zeros_like(sums_ref)
        gram_ref[...] = jnp.zeros_like(gram_ref)
        lean_ref[...] = jnp.zeros_like(lean_ref)

    width = first_ref.shape[1]
    latents = enc_ref.shape[0]
    weights[:latents, :] = enc_ref[...]
    weights[latents:, :] = dec_ref[...]
    gram_ref[...] += lax.dot_general(
        dec_ref[...], dec_ref[...], (((1,), (1,)), ((), ())), preferred_element_type=jnp.float32
    )
    lean = dec_ref[...].astype(jnp.float32) * bias_ref[...]
    for i in range(width // 128):
        lean_ref[...] += lean[:, i * 128:(i + 1) * 128]
    total = jnp.zeros(sums_ref.shape, jnp.float32)
    for i in range(width // unit):
        here = slice(i * unit, (i + 1) * unit)
        ids = lax.broadcasted_iota(jnp.int32, (residues, unit), 0)
        choice = (
            jnp.where(ids == second_ref[:, here], 1.0, 0.0) - jnp.where(ids == first_ref[:, here], 1.0, 0.0)
        ).astype(jnp.bfloat16)
        choice = jnp.concatenate([choice] * pieces, axis=0)
        square = jnp.zeros((rows, unit), jnp.float32)
        for axis in range(3):
            offset = jnp.dot(
                table[axis * rows:(axis + 1) * rows, :], choice, preferred_element_type=jnp.float32
            )
            square = square + offset * offset
        distance = square * lax.rsqrt(jnp.maximum(square, 1e-30))
        power = jnp.exp2(distance * (log2_e / softness) - cutoff_dist * log2_e / softness)
        contact = (1.0 / (1.0 + power)).astype(jnp.bfloat16)
        contact_ref[:, here] = contact
        total = total + lax.dot_general(
            contact, weights[:, here], (((1,), (1,)), ((), ())), preferred_element_type=jnp.float32
        )
    sums_ref[...] += total

    @pl.when(step == pl.num_programs(0) - 1)
    def finish():
        parts = out_ref.shape[0]
        part, few = rows // parts, latents // parts
        lean = jnp.broadcast_to(jnp.sum(lean_ref[...], axis=1, keepdims=True), (latents, latents))
        small = jnp.concatenate([gram_ref[...], lean], axis=1)
        for i in range(parts):
            out_ref[i, :part] = sums_ref[i * part:(i + 1) * part, :]
            out_ref[i, part:] = small[i * few:(i + 1) * few]


def contacts(coords, first, second, enc_weight, dec_weight, dec_bias):
    rows, _, residues = coords.shape
    latents, pairs = enc_weight.shape
    width = min(512, pairs)
    parts = lax.axis_size("pairs")
    sent = (parts, (rows + latents) // parts, 2 * latents)
    row = pl.BlockSpec((1, width), lambda i: (0, i))
    block = pl.BlockSpec((latents, width), lambda i: (0, i))
    return pl.pallas_call(
        contact_kernel,
        grid=(pairs // width,),
        in_specs=[pl.BlockSpec((3, rows, residues), lambda i: (0, 0, 0)), row, row, block, block, row],
        out_specs=[
            pl.BlockSpec((rows, width), lambda i: (0, i)),
            pl.BlockSpec(sent, lambda i: (0, 0, 0)),
        ],
        out_shape=[
            jax.ShapeDtypeStruct((rows, pairs), jnp.bfloat16),
            jax.ShapeDtypeStruct(sent, jnp.float32),
        ],
        scratch_shapes=[
            pltpu.VMEM((3 * rows, pieces * residues), jnp.bfloat16),
            pltpu.VMEM((2 * latents, width), jnp.bfloat16),
            pltpu.VMEM((rows, 2 * latents), jnp.float32),
            pltpu.VMEM((latents, latents), jnp.float32),
            pltpu.VMEM((latents, 128), jnp.float32),
        ],
        compiler_params=pltpu.CompilerParams(vmem_limit_bytes=50 * 2**20),
        cost_estimate=pl.CostEstimate(
            flops=2 * 3 * rows * pieces * residues * pairs,
            bytes_accessed=4 * rows * pairs,
            transcendentals=3 * rows * pairs,
        ),
        name="contacts",
    )(jnp.transpose(coords, (1, 0, 2)), first, second, enc_weight, dec_weight, dec_bias)


def encode(value, latents):
    size, width = value.shape[0], value.shape[-1]
    peaks = [
        jnp.maximum(jnp.max(jnp.max(jnp.abs(rows), axis=0), axis=0, keepdims=True), 1e-30)
        for rows in (value[:, :latents], value[:, latents:])
    ]
    both = lambda low, high, rows: jnp.concatenate(
        [jnp.broadcast_to(low, (rows, width)), jnp.broadcast_to(high, (rows, width))], axis=0
    )
    factor = both(32767.0 / peaks[0], 32767.0 / peaks[1], latents)
    codes = jnp.round(value * factor[None]).astype(jnp.int32).astype(jnp.int16)
    first_rows = lax.broadcasted_iota(jnp.int32, (8, width), 0) < 4
    steps = jnp.where(first_rows, peaks[0] * (1.0 / 32767.0), peaks[1] * (1.0 / 32767.0))
    return codes, steps


def decode(codes, steps, latents):
    width = steps.shape[-1]
    factor = jnp.concatenate(
        [jnp.broadcast_to(steps[:1], (latents, width)), jnp.broadcast_to(steps[4:5], (latents, width))], axis=0
    )
    return codes.astype(jnp.int32).astype(jnp.float32) * factor


def tail_kernel(
    chunks, lag_ref, scale_ref, enc_bias_ref, sums_ref, dec_ref, bias_ref, contact_any,
    out_ref, step_ref, contact_ref, zrecv, whole, seen_send, seen_recv, lat_send, lat_recv, left_ref,
    partial_sum, arrived, code_send, step_send, code_recv, step_recv,
    contact_sem, z_send, z_recv, side_send, side_recv, half_send, half_recv, full_send, full_recv,
):
    frames, pairs = lax.axis_size("frames"), lax.axis_size("pairs")
    me, depth = lax.axis_index("frames"), lax.axis_index("pairs")
    bits = frames.bit_length() - 1
    rows, latents = contact_any.shape[0], dec_ref.shape[0]
    part = rows // pairs
    width = dec_ref.shape[1] // chunks
    shard = width // frames
    half = rows // 2

    def partner(bit):
        return me + (1 << bit) - 2 * (1 << bit) * (lax.div(me, 1 << bit) % 2)

    def bit_of(bit):
        return lax.div(me, 1 << bit) % 2

    following, previous = lax.rem(me + 1, frames), lax.rem(me + frames - 1, frames)

    load = pltpu.make_async_copy(contact_any, contact_ref, contact_sem)
    load.start()
    barrier = pltpu.get_barrier_semaphore()
    for step in range(1, pairs):
        pl.semaphore_signal(
            barrier, inc=1, device_id={"pairs": lax.rem(depth + step, pairs)}, device_id_type=pl.DeviceIdType.MESH
        )
    for other in [following, previous] + [partner(b) for b in range(bits)]:
        pl.semaphore_signal(barrier, inc=1, device_id={"frames": other}, device_id_type=pl.DeviceIdType.MESH)
    pl.semaphore_wait(barrier, pairs - 1 + 2 + bits)

    scatter = []
    for step in range(1, pairs):
        other = lax.rem(depth + step, pairs)
        copy = pltpu.make_async_remote_copy(
            src_ref=sums_ref.at[other],
            dst_ref=zrecv.at[step - 1],
            send_sem=z_send.at[0, step - 1],
            recv_sem=z_recv.at[0, step - 1],
            device_id={"pairs": other},
            device_id_type=pl.DeviceIdType.MESH,
        )
        copy.start()
        scatter.append(copy)
    total = sums_ref[depth]
    for step in range(1, pairs):
        scatter[step - 1].wait_recv()
        total = total + zrecv[step - 1]
    whole[depth] = total
    gather = []
    for step in range(1, pairs):
        copy = pltpu.make_async_remote_copy(
            src_ref=whole.at[depth],
            dst_ref=whole.at[depth],
            send_sem=z_send.at[1, step - 1],
            recv_sem=z_recv.at[1, step - 1],
            device_id={"pairs": lax.rem(depth + step, pairs)},
            device_id_type=pl.DeviceIdType.MESH,
        )
        copy.start()
        gather.append(copy)
    for copy in gather:
        copy.wait_recv()

    sums = jnp.concatenate([whole[i, :part] for i in range(pairs)], axis=0)
    small = jnp.concatenate([whole[i, part:] for i in range(pairs)], axis=0)
    gram = small[:, :latents]
    lean = jnp.transpose(small)[latents:latents + 1, :]
    latent = jnp.tanh(sums[:, :latents] + enc_bias_ref[...])
    latent_bf = latent.astype(jnp.bfloat16)
    seen = sums[:, latents:]
    seen_send[...] = jnp.concatenate([seen[:half], seen[half:]], axis=1)
    lat_send[...] = jnp.concatenate([latent_bf[:half], latent_bf[half:]], axis=1)
    sides = []
    for i, (source, target, other) in enumerate(
        [(seen_send, seen_recv, previous), (lat_send, lat_recv, following)]
    ):
        copy = pltpu.make_async_remote_copy(
            src_ref=source,
            dst_ref=target,
            send_sem=side_send.at[i],
            recv_sem=side_recv.at[i],
            device_id={"frames": other},
            device_id_type=pl.DeviceIdType.MESH,
        )
        copy.start()
        sides.append(copy)

    lag = lag_ref[...]
    scale = scale_ref[...]
    frame = lax.broadcasted_iota(jnp.int32, (rows, 1), 0)
    usable = me * rows + frame + lag < rows * frames
    used = jnp.where(usable, latent_bf.astype(jnp.float32), 0.0).astype(jnp.bfloat16)
    mix = lax.dot_general(used, used, (((0,), (0,)), ((), ())), preferred_element_type=jnp.float32)
    tilt = lax.dot_general(
        used, jnp.ones((rows, 128), jnp.bfloat16), (((0,), (0,)), ((), ())), preferred_element_type=jnp.float32
    )[:, :1]
    mix_parts = jnp.concatenate(split(mix, 3), axis=1)
    decoded = lean
    for piece in split(gram, 3):
        decoded = decoded + jnp.dot(latent_bf, piece, preferred_element_type=jnp.float32)
    for copy in sides:
        copy.wait_recv()
    seen_all = jnp.concatenate([seen, seen_recv[:, :latents], seen_recv[:, latents:]], axis=0)
    latent_all = jnp.concatenate([lat_recv[:, :latents], lat_recv[:, latents:], latent_bf], axis=0)
    place = lax.broadcasted_iota(jnp.int32, (rows, 2 * rows), 1)
    pick_later = jnp.where(place == frame + lag, 1.0, 0.0).astype(jnp.bfloat16)
    pick_earlier = jnp.where(place == frame + rows - lag, 1.0, 0.0).astype(jnp.bfloat16)
    later = jnp.zeros((rows, latents), jnp.float32)
    for piece in split(seen_all, 3):
        later = later + jnp.dot(pick_later, piece, preferred_element_type=jnp.float32)
    earlier = jnp.dot(pick_earlier, latent_all, preferred_element_type=jnp.float32)
    earlier = jnp.where(me * rows + frame >= lag, earlier, 0.0)
    backward = jnp.where(usable, (decoded - later) * scale, 0.0)
    hidden = backward * (1.0 - latent * latent)
    left_ref[...] = jnp.transpose(jnp.concatenate([hidden, earlier], axis=1)).astype(jnp.bfloat16)
    load.wait()

    def order(color):
        turn = color % max(bits - 1, 1)
        later_bits = list(range(1, bits))
        return [0] + later_bits[turn:] + later_bits[:turn]

    def begin_of(sequence, count):
        begin = 0
        for k in range(count):
            begin = begin + bit_of(sequence[k]) * (frames >> (k + 1))
        return begin

    def remote(source, target, sender, receiver, bit):
        return pltpu.make_async_remote_copy(
            src_ref=source,
            dst_ref=target,
            send_sem=sender,
            recv_sem=receiver,
            device_id={"frames": partner(bit)},
            device_id_type=pl.DeviceIdType.MESH,
        )

    def halving(chunk, sequence, k):
        size = frames >> (k + 1)
        if k == 0:
            begin = (1 - bit_of(sequence[0])) * size
            return [
                remote(
                    partial_sum.at[chunk, pl.ds(begin, size)], arrived.at[chunk],
                    half_send.at[0, chunk, k], half_recv.at[0, chunk, k], sequence[k],
                )
            ]
        here = pl.ds(frames // 2 - 2 * size, size)
        return [
            remote(
                code_send.at[chunk, here], code_recv.at[chunk, here],
                half_send.at[0, chunk, k], half_recv.at[0, chunk, k], sequence[k],
            ),
            remote(
                step_send.at[chunk, k - 1], step_recv.at[chunk, k - 1],
                half_send.at[1, chunk, k], half_recv.at[1, chunk, k], sequence[k],
            ),
        ]

    def doubling(chunk, sequence, k):
        here = pl.ds(begin_of(sequence, k + 1), frames >> (k + 1))
        return [
            remote(
                ref.at[chunk, here], ref.at[chunk, here],
                full_send.at[i, chunk, k], full_recv.at[i, chunk, k], sequence[k],
            )
            for i, ref in enumerate((out_ref, step_ref))
        ]

    def each_chunk(body):
        def pair(index, carry):
            for color in range(2):
                body(index * 2 + color, order(color))
            return carry

        lax.fori_loop(0, chunks // 2, pair, 0)

    def multiply(chunk, sequence):
        columns = pl.ds(pl.multiple_of(chunk * width, width), width)
        product = jnp.dot(left_ref[...], contact_ref[:, columns], preferred_element_type=jnp.float32)
        dec = dec_ref[:, columns]
        own = jnp.dot(mix_parts, jnp.concatenate([dec, dec, dec], axis=0), preferred_element_type=jnp.float32)
        decode = scale * (own + tilt * bias_ref[:, columns] - product[latents:])
        for i in range(frames):
            here = slice(i * shard, (i + 1) * shard)
            partial_sum[chunk, i, :latents] = product[:latents, here]
            partial_sum[chunk, i, latents:] = decode[:, here]
        for copy in halving(chunk, sequence, 0):
            copy.start()

    each_chunk(multiply)
    for k in range(bits):
        def reduce(chunk, sequence, k=k):
            for copy in halving(chunk, sequence, k):
                copy.wait_recv()
            size = frames >> (k + 1)
            begin = begin_of(sequence, k + 1)
            if k == 0:
                came = arrived[chunk]
            else:
                codes = code_recv[chunk, pl.ds(frames // 2 - 2 * size, size)]
                came = decode(codes, step_recv[chunk, k - 1], latents)
            added = partial_sum[chunk, pl.ds(begin, size)] + came
            if k < bits - 1:
                half_size = size // 2
                turn = bit_of(sequence[k + 1])
                partial_sum[chunk, pl.ds(begin, size)] = added
                leaving = partial_sum[chunk, pl.ds(begin + (1 - turn) * half_size, half_size)]
                codes, steps = encode(leaving, latents)
                code_send[chunk, pl.ds(frames // 2 - 2 * half_size, half_size)] = codes
                step_send[chunk, k] = steps
                for copy in halving(chunk, sequence, k + 1):
                    copy.start()
            else:
                codes, steps = encode(added, latents)
                out_ref[chunk, pl.ds(begin, 1)] = codes
                step_ref[chunk, begin] = steps
                for copy in doubling(chunk, sequence, k):
                    copy.start()

        each_chunk(reduce)
    for k in reversed(range(bits)):
        def spread(chunk, sequence, k=k):
            for copy in doubling(chunk, sequence, k):
                copy.wait_recv()
            if k > 0:
                for copy in doubling(chunk, sequence, k - 1):
                    copy.start()

        each_chunk(spread)

    def finish(chunk, sequence):
        for k in range(bits):
            for copy in halving(chunk, sequence, k) + doubling(chunk, sequence, k):
                copy.wait_send()

    each_chunk(finish)
    for copy in scatter + gather + sides:
        copy.wait_send()


def tail(lag, scale, enc_bias, sums, dec_weight, dec_bias, contact):
    rows, pairs = contact.shape
    latents = dec_weight.shape[0]
    frames, depth = lax.axis_size("frames"), lax.axis_size("pairs")
    bits = frames.bit_length() - 1
    chunks = 2 * max(1, min(4, pairs // (2 * frames * 128)))
    shard = pairs // chunks // frames
    vmem = pl.BlockSpec(memory_space=pltpu.VMEM)
    dma = pltpu.SemaphoreType.DMA
    return pl.pallas_call(
        partial(tail_kernel, chunks),
        in_specs=[vmem] * 6 + [pl.BlockSpec(memory_space=pl.ANY)],
        out_specs=[vmem, vmem],
        out_shape=[
            jax.ShapeDtypeStruct((chunks, frames, 2 * latents, shard), jnp.int16),
            jax.ShapeDtypeStruct((chunks, frames, 8, shard), jnp.float32),
        ],
        scratch_shapes=[
            pltpu.VMEM((rows, pairs), jnp.bfloat16),
            pltpu.VMEM((depth - 1, *sums.shape[1:]), jnp.float32),
            pltpu.VMEM(sums.shape, jnp.float32),
            pltpu.VMEM((rows // 2, 2 * latents), jnp.float32),
            pltpu.VMEM((rows // 2, 2 * latents), jnp.float32),
            pltpu.VMEM((rows // 2, 2 * latents), jnp.bfloat16),
            pltpu.VMEM((rows // 2, 2 * latents), jnp.bfloat16),
            pltpu.VMEM((2 * latents, rows), jnp.bfloat16),
            pltpu.VMEM((chunks, frames, 2 * latents, shard), jnp.float32),
            pltpu.VMEM((chunks, frames // 2, 2 * latents, shard), jnp.float32),
            pltpu.VMEM((chunks, max(1, frames // 2 - 1), 2 * latents, shard), jnp.int16),
            pltpu.VMEM((chunks, max(1, bits - 1), 8, shard), jnp.float32),
            pltpu.VMEM((chunks, max(1, frames // 2 - 1), 2 * latents, shard), jnp.int16),
            pltpu.VMEM((chunks, max(1, bits - 1), 8, shard), jnp.float32),
            dma,
            dma((2, depth - 1)),
            dma((2, depth - 1)),
            dma((2,)),
            dma((2,)),
            dma((2, chunks, bits)),
            dma((2, chunks, bits)),
            dma((2, chunks, bits)),
            dma((2, chunks, bits)),
        ],
        compiler_params=pltpu.CompilerParams(
            vmem_limit_bytes=50 * 2**20, collective_id=0, has_side_effects=True
        ),
        name="tail",
    )(lag, scale, enc_bias, sums, dec_weight, dec_bias, contact)


def decode_kernel(code_ref, step_ref, enc_out, dec_out):
    frames, shard = code_ref.shape[1], code_ref.shape[3]
    latents = enc_out.shape[0]
    for i in range(frames):
        value = decode(code_ref[0, i], step_ref[0, i], latents)
        enc_out[:, i * shard:(i + 1) * shard] = value[:latents]
        dec_out[:, i * shard:(i + 1) * shard] = value[latents:]


def decoded_outputs(codes, steps):
    chunks, frames, rows, shard = codes.shape
    latents, width = rows // 2, frames * shard
    out = pl.BlockSpec((latents, width), lambda i: (0, i))
    return pl.pallas_call(
        decode_kernel,
        grid=(chunks,),
        in_specs=[
            pl.BlockSpec((1, frames, rows, shard), lambda i: (i, 0, 0, 0)),
            pl.BlockSpec((1, frames, 8, shard), lambda i: (i, 0, 0, 0)),
        ],
        out_specs=[out, out],
        out_shape=[jax.ShapeDtypeStruct((latents, chunks * width), jnp.float32)] * 2,
        name="decode",
    )(codes, steps)


def local(coords, pair_first, pair_second, enc_weight, enc_bias, dec_weight, dec_bias, lag_frames):
    rows = coords.shape[0]
    latents, pairs = enc_weight.shape
    total_frames = rows * lax.axis_size("frames")
    first = jnp.broadcast_to(pair_first[:, None], (pairs // 128, 128)).reshape(1, pairs)
    bias = dec_bias.reshape(1, pairs)
    contact, sums = contacts(coords, first, pair_second.reshape(1, pairs), enc_weight, dec_weight, bias)
    scale = 1.0 / jnp.sqrt(jnp.float32(total_frames) - lag_frames.astype(jnp.float32))
    codes, steps = tail(
        lag_frames.reshape(1, 1), scale.reshape(1, 1), enc_bias.reshape(1, latents), sums,
        dec_weight, bias, contact,
    )
    return tuple(decoded_outputs(codes, steps))


def solution(mesh):
    placed = (
        P("frames", None, None),
        P("pairs"),
        P("pairs"),
        P(None, "pairs"),
        P(),
        P(None, "pairs"),
        P("pairs"),
        P(),
    )
    return jax.shard_map(
        local,
        mesh=mesh,
        in_specs=placed,
        out_specs=(P(None, "pairs"), P(None, "pairs")),
        check_vma=False,
    )
```

```python
from functools import partial

import jax
import jax.numpy as jnp
from jax import lax
from jax.experimental import pallas as pl
from jax.experimental.pallas import tpu as pltpu
from jax.sharding import PartitionSpec as P

cutoff_dist = 2.3
softness = 0.4
log2_e = 1.4426950408889634
pieces = 2
unit = 256


def split(value, count):
    parts = []
    rest = value
    for _ in range(count):
        part = rest.astype(jnp.bfloat16)
        parts.append(part)
        rest = rest - part.astype(jnp.float32)
    return parts


def contact_kernel(
    coords_ref, first_ref, second_ref, enc_ref, dec_ref, bias_ref, contact_ref, out_ref, table, weights,
    sums_ref, gram_ref, lean_ref,

):
    step = pl.program_id(0)
    rows, residues = coords_ref.shape[1], coords_ref.shape[2]

    @pl.when(step == 0)
    def prepare():
        for axis in range(3):
            for i, part in enumerate(split(coords_ref[axis], pieces)):
                table[axis * rows:(axis + 1) * rows, i * residues:(i + 1) * residues] = part
        sums_ref[...] = jnp.zeros_like(sums_ref)
        gram_ref[...] = jnp.zeros_like(gram_ref)
        lean_ref[...] = jnp.zeros_like(lean_ref)

    width = second_ref.shape[1]
    latents = enc_ref.shape[0]
    weights[:latents, :] = enc_ref[...]
    weights[latents:, :] = dec_ref[...]
    gram_ref[...] += lax.dot_general(
        dec_ref[...], dec_ref[...], (((1,), (1,)), ((), ())), preferred_element_type=jnp.float32
    )
    lean = dec_ref[...].astype(jnp.float32) * bias_ref[...]
    for i in range(width // 128):
        lean_ref[...] += lean[:, i * 128:(i + 1) * 128]
    total = jnp.zeros(sums_ref.shape, jnp.float32)
    for i in range(width // unit):
        here = slice(i * unit, (i + 1) * unit)
        ids = lax.broadcasted_iota(jnp.int32, (residues, unit), 0)
        near = jnp.concatenate(
            [
                jnp.where(ids[:, :128] == first_ref[(step * width + i * unit) // 128 + j], 1.0, 0.0)
                for j in range(unit // 128)
            ],
            axis=1,
        )
        choice = (jnp.where(ids == second_ref[:, here], 1.0, 0.0) - near).astype(jnp.bfloat16)
        choice = jnp.concatenate([choice] * pieces, axis=0)
        square = jnp.zeros((rows, unit), jnp.float32)
        for axis in range(3):
            offset = jnp.dot(
                table[axis * rows:(axis + 1) * rows, :], choice, preferred_element_type=jnp.float32
            )
            square = square + offset * offset
        distance = square * lax.rsqrt(jnp.maximum(square, 1e-30))
        power = jnp.exp2(distance * (log2_e / softness) - cutoff_dist * log2_e / softness)
        contact = pltpu.reciprocal(1.0 + power, approx=True).astype(jnp.bfloat16)
        contact_ref[:, here] = contact
        total = total + lax.dot_general(
            contact, weights[:, here], (((1,), (1,)), ((), ())), preferred_element_type=jnp.float32
        )
    sums_ref[...] += total

    @pl.when(step == pl.num_programs(0) - 1)
    def finish():
        parts = out_ref.shape[0]
        part, few = rows // parts, latents // parts
        lean = jnp.broadcast_to(jnp.sum(lean_ref[...], axis=1, keepdims=True), (latents, latents))
        small = jnp.concatenate([gram_ref[...], lean], axis=1)
        for i in range(parts):
            out_ref[i, :part] = sums_ref[i * part:(i + 1) * part, :]
            out_ref[i, part:] = small[i * few:(i + 1) * few]


def contacts(coords, first, second, enc_weight, dec_weight, dec_bias):
    rows, _, residues = coords.shape
    latents, pairs = enc_weight.shape
    width = min(2048, pairs)
    parts = lax.axis_size("pairs")
    sent = (parts, (rows + latents) // parts, 2 * latents)
    row = pl.BlockSpec((1, width), lambda i: (0, i))
    block = pl.BlockSpec((latents, width), lambda i: (0, i))
    return pl.pallas_call(
        contact_kernel,
        grid=(pairs // width,),
        in_specs=[pl.BlockSpec((3, rows, residues), lambda i: (0, 0, 0)), pl.BlockSpec(memory_space=pltpu.SMEM), row, block, block, row],
        out_specs=[
            pl.BlockSpec((rows, width), lambda i: (0, i)),
            pl.BlockSpec(sent, lambda i: (0, 0, 0)),
        ],
        out_shape=[
            jax.ShapeDtypeStruct((rows, pairs), jnp.bfloat16),
            jax.ShapeDtypeStruct(sent, jnp.float32),
        ],
        scratch_shapes=[
            pltpu.VMEM((3 * rows, pieces * residues), jnp.bfloat16),
            pltpu.VMEM((2 * latents, width), jnp.bfloat16),
            pltpu.VMEM((rows, 2 * latents), jnp.float32),
            pltpu.VMEM((latents, latents), jnp.float32),
            pltpu.VMEM((latents, 128), jnp.float32),
        ],
        compiler_params=pltpu.CompilerParams(vmem_limit_bytes=60 * 2**20),
        cost_estimate=pl.CostEstimate(
            flops=2 * 3 * rows * pieces * residues * pairs,
            bytes_accessed=4 * rows * pairs,
            transcendentals=3 * rows * pairs,
        ),
        name="contacts",
    )(jnp.transpose(coords, (1, 0, 2)), first, second, enc_weight, dec_weight, dec_bias)


def encode(value, latents):
    size, width = value.shape[0], value.shape[-1]
    peaks = [
        jnp.maximum(jnp.max(jnp.max(jnp.abs(rows), axis=0), axis=0, keepdims=True), 1e-30)
        for rows in (value[:, :latents], value[:, latents:])
    ]
    both = lambda low, high, rows: jnp.concatenate(
        [jnp.broadcast_to(low, (rows, width)), jnp.broadcast_to(high, (rows, width))], axis=0
    )
    factor = both(32767.0 / peaks[0], 32767.0 / peaks[1], latents)
    codes = jnp.round(value * factor[None]).astype(jnp.int32).astype(jnp.int16)
    first_rows = lax.broadcasted_iota(jnp.int32, (8, width), 0) < 4
    steps = jnp.where(first_rows, peaks[0] * (1.0 / 32767.0), peaks[1] * (1.0 / 32767.0))
    return codes, steps


def decode(codes, steps, latents):
    width = steps.shape[-1]
    factor = jnp.concatenate(
        [jnp.broadcast_to(steps[:1], (latents, width)), jnp.broadcast_to(steps[4:5], (latents, width))], axis=0
    )
    return codes.astype(jnp.int32).astype(jnp.float32) * factor


def tail_kernel(
    chunks, lag_ref, scale_ref, enc_bias_ref, sums_ref, dec_ref, bias_ref, contact_any,
    out_ref, step_ref, contact_ref, zrecv, whole, seen_send, seen_recv, lat_send, lat_recv, left_ref,
    partial_sum, arrived, code_send, step_send, code_recv, step_recv,
    contact_sem, z_send, z_recv, side_send, side_recv, half_send, half_recv, full_send, full_recv,
):
    frames, pairs = lax.axis_size("frames"), lax.axis_size("pairs")
    me, depth = lax.axis_index("frames"), lax.axis_index("pairs")
    bits = frames.bit_length() - 1
    rows, latents = contact_any.shape[0], dec_ref.shape[0]
    part = rows // pairs
    width = dec_ref.shape[1] // chunks
    shard = width // frames
    half = rows // 2

    def partner(bit):
        return me + (1 << bit) - 2 * (1 << bit) * (lax.div(me, 1 << bit) % 2)

    def bit_of(bit):
        return lax.div(me, 1 << bit) % 2

    following, previous = lax.rem(me + 1, frames), lax.rem(me + frames - 1, frames)

    load = pltpu.make_async_copy(contact_any, contact_ref, contact_sem)
    load.start()
    barrier = pltpu.get_barrier_semaphore()
    for step in range(1, pairs):
        pl.semaphore_signal(
            barrier, inc=1, device_id={"pairs": lax.rem(depth + step, pairs)}, device_id_type=pl.DeviceIdType.MESH
        )
    for other in [following, previous] + [partner(b) for b in range(bits)]:
        pl.semaphore_signal(barrier, inc=1, device_id={"frames": other}, device_id_type=pl.DeviceIdType.MESH)
    pl.semaphore_wait(barrier, pairs - 1 + 2 + bits)

    scatter = []
    for step in range(1, pairs):
        other = lax.rem(depth + step, pairs)
        copy = pltpu.make_async_remote_copy(
            src_ref=sums_ref.at[other],
            dst_ref=zrecv.at[step - 1],
            send_sem=z_send.at[0, step - 1],
            recv_sem=z_recv.at[0, step - 1],
            device_id={"pairs": other},
            device_id_type=pl.DeviceIdType.MESH,
        )
        copy.start()
        scatter.append(copy)
    total = sums_ref[depth]
    for step in range(1, pairs):
        scatter[step - 1].wait_recv()
        total = total + zrecv[step - 1]
    whole[depth] = total
    gather = []
    for step in range(1, pairs):
        copy = pltpu.make_async_remote_copy(
            src_ref=whole.at[depth],
            dst_ref=whole.at[depth],
            send_sem=z_send.at[1, step - 1],
            recv_sem=z_recv.at[1, step - 1],
            device_id={"pairs": lax.rem(depth + step, pairs)},
            device_id_type=pl.DeviceIdType.MESH,
        )
        copy.start()
        gather.append(copy)
    for copy in gather:
        copy.wait_recv()

    sums = jnp.concatenate([whole[i, :part] for i in range(pairs)], axis=0)
    small = jnp.concatenate([whole[i, part:] for i in range(pairs)], axis=0)
    gram = small[:, :latents]
    lean = jnp.transpose(small)[latents:latents + 1, :]
    latent = jnp.tanh(sums[:, :latents] + enc_bias_ref[...])
    latent_bf = latent.astype(jnp.bfloat16)
    seen = sums[:, latents:]
    seen_send[...] = jnp.concatenate([seen[:half], seen[half:]], axis=1)
    lat_send[...] = jnp.concatenate([latent_bf[:half], latent_bf[half:]], axis=1)
    sides = []
    for i, (source, target, other) in enumerate(
        [(seen_send, seen_recv, previous), (lat_send, lat_recv, following)]
    ):
        copy = pltpu.make_async_remote_copy(
            src_ref=source,
            dst_ref=target,
            send_sem=side_send.at[i],
            recv_sem=side_recv.at[i],
            device_id={"frames": other},
            device_id_type=pl.DeviceIdType.MESH,
        )
        copy.start()
        sides.append(copy)

    lag = lag_ref[...]
    scale = scale_ref[...]
    frame = lax.broadcasted_iota(jnp.int32, (rows, 1), 0)
    usable = me * rows + frame + lag < rows * frames
    used = jnp.where(usable, latent_bf.astype(jnp.float32), 0.0).astype(jnp.bfloat16)
    mix = lax.dot_general(used, used, (((0,), (0,)), ((), ())), preferred_element_type=jnp.float32)
    tilt = lax.dot_general(
        used, jnp.ones((rows, 128), jnp.bfloat16), (((0,), (0,)), ((), ())), preferred_element_type=jnp.float32
    )[:, :1]
    mix_parts = jnp.concatenate(split(mix, 3), axis=1)
    decoded = lean
    for piece in split(gram, 3):
        decoded = decoded + jnp.dot(latent_bf, piece, preferred_element_type=jnp.float32)
    for copy in sides:
        copy.wait_recv()
    seen_all = jnp.concatenate([seen, seen_recv[:, :latents], seen_recv[:, latents:]], axis=0)
    latent_all = jnp.concatenate([lat_recv[:, :latents], lat_recv[:, latents:], latent_bf], axis=0)
    place = lax.broadcasted_iota(jnp.int32, (rows, 2 * rows), 1)
    pick_later = jnp.where(place == frame + lag, 1.0, 0.0).astype(jnp.bfloat16)
    pick_earlier = jnp.where(place == frame + rows - lag, 1.0, 0.0).astype(jnp.bfloat16)
    later = jnp.zeros((rows, latents), jnp.float32)
    for piece in split(seen_all, 3):
        later = later + jnp.dot(pick_later, piece, preferred_element_type=jnp.float32)
    earlier = jnp.dot(pick_earlier, latent_all, preferred_element_type=jnp.float32)
    earlier = jnp.where(me * rows + frame >= lag, earlier, 0.0)
    backward = jnp.where(usable, (decoded - later) * scale, 0.0)
    hidden = backward * (1.0 - latent * latent)
    left_ref[...] = jnp.transpose(jnp.concatenate([hidden, earlier], axis=1)).astype(jnp.bfloat16)
    load.wait()

    def order(color):
        turn = color % max(bits - 1, 1)
        later_bits = list(range(1, bits))
        return [0] + later_bits[turn:] + later_bits[:turn]

    def begin_of(sequence, count):
        begin = 0
        for k in range(count):
            begin = begin + bit_of(sequence[k]) * (frames >> (k + 1))
        return begin

    def remote(source, target, sender, receiver, bit):
        return pltpu.make_async_remote_copy(
            src_ref=source,
            dst_ref=target,
            send_sem=sender,
            recv_sem=receiver,
            device_id={"frames": partner(bit)},
            device_id_type=pl.DeviceIdType.MESH,
        )

    def halving(chunk, sequence, k):
        size = frames >> (k + 1)
        if k == 0:
            begin = (1 - bit_of(sequence[0])) * size
            return [
                remote(
                    partial_sum.at[chunk, pl.ds(begin, size)], arrived.at[chunk],
                    half_send.at[0, chunk, k], half_recv.at[0, chunk, k], sequence[k],
                )
            ]
        here = pl.ds(frames // 2 - 2 * size, size)
        return [
            remote(
                code_send.at[chunk, here], code_recv.at[chunk, here],
                half_send.at[0, chunk, k], half_recv.at[0, chunk, k], sequence[k],
            ),
            remote(
                step_send.at[chunk, k - 1], step_recv.at[chunk, k - 1],
                half_send.at[1, chunk, k], half_recv.at[1, chunk, k], sequence[k],
            ),
        ]

    def doubling(chunk, sequence, k):
        here = pl.ds(begin_of(sequence, k + 1), frames >> (k + 1))
        return [
            remote(
                ref.at[chunk, here], ref.at[chunk, here],
                full_send.at[i, chunk, k], full_recv.at[i, chunk, k], sequence[k],
            )
            for i, ref in enumerate((out_ref, step_ref))
        ]

    def each_chunk(body):
        def pair(index, carry):
            for color in range(2):
                body(index * 2 + color, order(color))
            return carry

        lax.fori_loop(0, chunks // 2, pair, 0)

    def multiply(chunk, sequence):
        columns = pl.ds(pl.multiple_of(chunk * width, width), width)
        product = jnp.dot(left_ref[...], contact_ref[:, columns], preferred_element_type=jnp.float32)
        dec = dec_ref[:, columns]
        own = jnp.dot(mix_parts, jnp.concatenate([dec, dec, dec], axis=0), preferred_element_type=jnp.float32)
        decode = scale * (own + tilt * bias_ref[:, columns] - product[latents:])
        for i in range(frames):
            here = slice(i * shard, (i + 1) * shard)
            partial_sum[chunk, i, :latents] = product[:latents, here]
            partial_sum[chunk, i, latents:] = decode[:, here]
        for copy in halving(chunk, sequence, 0):
            copy.start()

    each_chunk(multiply)
    for k in range(bits):
        def reduce(chunk, sequence, k=k):
            for copy in halving(chunk, sequence, k):
                copy.wait_recv()
            size = frames >> (k + 1)
            begin = begin_of(sequence, k + 1)
            if k == 0:
                came = arrived[chunk]
            else:
                codes = code_recv[chunk, pl.ds(frames // 2 - 2 * size, size)]
                came = decode(codes, step_recv[chunk, k - 1], latents)
            added = partial_sum[chunk, pl.ds(begin, size)] + came
            if k < bits - 1:
                half_size = size // 2
                turn = bit_of(sequence[k + 1])
                partial_sum[chunk, pl.ds(begin, size)] = added
                leaving = partial_sum[chunk, pl.ds(begin + (1 - turn) * half_size, half_size)]
                codes, steps = encode(leaving, latents)
                code_send[chunk, pl.ds(frames // 2 - 2 * half_size, half_size)] = codes
                step_send[chunk, k] = steps
                for copy in halving(chunk, sequence, k + 1):
                    copy.start()
            else:
                codes, steps = encode(added, latents)
                out_ref[chunk, pl.ds(begin, 1)] = codes
                step_ref[chunk, begin] = steps
                for copy in doubling(chunk, sequence, k):
                    copy.start()

        each_chunk(reduce)
    for k in reversed(range(bits)):
        def spread(chunk, sequence, k=k):
            for copy in doubling(chunk, sequence, k):
                copy.wait_recv()
            if k > 0:
                for copy in doubling(chunk, sequence, k - 1):
                    copy.start()

        each_chunk(spread)

    def finish(chunk, sequence):
        for k in range(bits):
            for copy in halving(chunk, sequence, k) + doubling(chunk, sequence, k):
                copy.wait_send()

    each_chunk(finish)
    for copy in scatter + gather + sides:
        copy.wait_send()


def tail(lag, scale, enc_bias, sums, dec_weight, dec_bias, contact):
    rows, pairs = contact.shape
    latents = dec_weight.shape[0]
    frames, depth = lax.axis_size("frames"), lax.axis_size("pairs")
    bits = frames.bit_length() - 1
    chunks = 2 * max(1, min(4, pairs // (2 * frames * 128)))
    shard = pairs // chunks // frames
    vmem = pl.BlockSpec(memory_space=pltpu.VMEM)
    dma = pltpu.SemaphoreType.DMA
    return pl.pallas_call(
        partial(tail_kernel, chunks),
        in_specs=[vmem] * 6 + [pl.BlockSpec(memory_space=pl.ANY)],
        out_specs=[vmem, vmem],
        out_shape=[
            jax.ShapeDtypeStruct((chunks, frames, 2 * latents, shard), jnp.int16),
            jax.ShapeDtypeStruct((chunks, frames, 8, shard), jnp.float32),
        ],
        scratch_shapes=[
            pltpu.VMEM((rows, pairs), jnp.bfloat16),
            pltpu.VMEM((depth - 1, *sums.shape[1:]), jnp.float32),
            pltpu.VMEM(sums.shape, jnp.float32),
            pltpu.VMEM((rows // 2, 2 * latents), jnp.float32),
            pltpu.VMEM((rows // 2, 2 * latents), jnp.float32),
            pltpu.VMEM((rows // 2, 2 * latents), jnp.bfloat16),
            pltpu.VMEM((rows // 2, 2 * latents), jnp.bfloat16),
            pltpu.VMEM((2 * latents, rows), jnp.bfloat16),
            pltpu.VMEM((chunks, frames, 2 * latents, shard), jnp.float32),
            pltpu.VMEM((chunks, frames // 2, 2 * latents, shard), jnp.float32),
            pltpu.VMEM((chunks, max(1, frames // 2 - 1), 2 * latents, shard), jnp.int16),
            pltpu.VMEM((chunks, max(1, bits - 1), 8, shard), jnp.float32),
            pltpu.VMEM((chunks, max(1, frames // 2 - 1), 2 * latents, shard), jnp.int16),
            pltpu.VMEM((chunks, max(1, bits - 1), 8, shard), jnp.float32),
            dma,
            dma((2, depth - 1)),
            dma((2, depth - 1)),
            dma((2,)),
            dma((2,)),
            dma((2, chunks, bits)),
            dma((2, chunks, bits)),
            dma((2, chunks, bits)),
            dma((2, chunks, bits)),
        ],
        compiler_params=pltpu.CompilerParams(
            vmem_limit_bytes=60 * 2**20, collective_id=0, has_side_effects=True
        ),
        name="tail",
    )(lag, scale, enc_bias, sums, dec_weight, dec_bias, contact)


def decode_kernel(code_ref, step_ref, enc_out, dec_out, values, sems):
    chunks, frames, rows, shard = code_ref.shape
    latents, width = rows // 2, frames * shard

    def leave(chunk):
        here = pl.ds(pl.multiple_of(chunk * width, width), width)
        return [
            pltpu.make_async_copy(values.at[chunk, i], out.at[:, here], sems.at[i, chunk])
            for i, out in enumerate((enc_out, dec_out))
        ]

    def one(chunk, carry):
        for i in range(frames):
            value = decode(code_ref[chunk, i], step_ref[chunk, i], latents)
            values[chunk, 0, :, i * shard:(i + 1) * shard] = value[:latents]
            values[chunk, 1, :, i * shard:(i + 1) * shard] = value[latents:]
        for copy in leave(chunk):
            copy.start()
        return carry

    lax.fori_loop(0, chunks, one, 0)

    def end(chunk, carry):
        for copy in leave(chunk):
            copy.wait()
        return carry

    lax.fori_loop(0, chunks, end, 0)


def decoded_outputs(codes, steps):
    chunks, frames, rows, shard = codes.shape
    latents, width = rows // 2, frames * shard
    return pl.pallas_call(
        decode_kernel,
        in_specs=[pl.BlockSpec(memory_space=pltpu.VMEM)] * 2,
        out_specs=[pl.BlockSpec(memory_space=pl.ANY)] * 2,
        out_shape=[jax.ShapeDtypeStruct((latents, chunks * width), jnp.float32)] * 2,
        scratch_shapes=[
            pltpu.VMEM((chunks, 2, latents, width), jnp.float32),
            pltpu.SemaphoreType.DMA((2, chunks)),
        ],
        compiler_params=pltpu.CompilerParams(vmem_limit_bytes=24 * 2**20),
        name="decode",
    )(codes, steps)


def local(coords, pair_first, pair_second, enc_weight, enc_bias, dec_weight, dec_bias, lag_frames):
    rows = coords.shape[0]
    latents, pairs = enc_weight.shape
    total_frames = rows * lax.axis_size("frames")
    bias = dec_bias.reshape(1, pairs)
    contact, sums = contacts(coords, pair_first, pair_second.reshape(1, pairs), enc_weight, dec_weight, bias)
    scale = 1.0 / jnp.sqrt(jnp.float32(total_frames) - lag_frames.astype(jnp.float32))
    codes, steps = tail(
        lag_frames.reshape(1, 1), scale.reshape(1, 1), enc_bias.reshape(1, latents), sums,
        dec_weight, bias, contact,
    )
    return tuple(decoded_outputs(codes, steps))


def solution(mesh):
    placed = (
        P("frames", None, None),
        P("pairs"),
        P("pairs"),
        P(None, "pairs"),
        P(),
        P(None, "pairs"),
        P("pairs"),
        P(),
    )
    return jax.shard_map(
        local,
        mesh=mesh,
        in_specs=placed,
        out_specs=(P(None, "pairs"), P(None, "pairs")),
        check_vma=False,
    )
```

```python
from functools import partial

import jax
import jax.numpy as jnp
from jax import lax
from jax.experimental import pallas as pl
from jax.experimental.pallas import tpu as pltpu
from jax.sharding import PartitionSpec as P

cutoff_dist = 2.3
softness = 0.4
log2_e = 1.4426950408889634
pieces = 2
unit = 256


def split(value, count):
    parts = []
    rest = value
    for _ in range(count):
        part = rest.astype(jnp.bfloat16)
        parts.append(part)
        rest = rest - part.astype(jnp.float32)
    return parts


def contact_kernel(
    coords_ref, first_ref, second_ref, enc_ref, dec_ref, bias_ref, contact_ref, out_ref, table, weights,
    sums_ref, gram_ref, lean_ref,

):
    step = pl.program_id(0)
    rows, residues = coords_ref.shape[1], coords_ref.shape[2]

    @pl.when(step == 0)
    def prepare():
        for axis in range(3):
            for i, part in enumerate(split(coords_ref[axis], pieces)):
                table[axis * rows:(axis + 1) * rows, i * residues:(i + 1) * residues] = part
        sums_ref[...] = jnp.zeros_like(sums_ref)
        gram_ref[...] = jnp.zeros_like(gram_ref)
        lean_ref[...] = jnp.zeros_like(lean_ref)

    width = second_ref.shape[1]
    latents = enc_ref.shape[0]
    weights[:latents, :] = enc_ref[...]
    weights[latents:, :] = dec_ref[...]
    gram_ref[...] += lax.dot_general(
        dec_ref[...], dec_ref[...], (((1,), (1,)), ((), ())), preferred_element_type=jnp.float32
    )
    lean = dec_ref[...].astype(jnp.float32) * bias_ref[...]
    for i in range(width // 128):
        lean_ref[...] += lean[:, i * 128:(i + 1) * 128]
    total = jnp.zeros(sums_ref.shape, jnp.float32)
    for i in range(width // unit):
        here = slice(i * unit, (i + 1) * unit)
        ids = lax.broadcasted_iota(jnp.int32, (residues, unit), 0)
        near = jnp.concatenate(
            [
                jnp.where(ids[:, :128] == first_ref[(step * width + i * unit) // 128 + j], 1.0, 0.0)
                for j in range(unit // 128)
            ],
            axis=1,
        )
        choice = (jnp.where(ids == second_ref[:, here], 1.0, 0.0) - near).astype(jnp.bfloat16)
        choice = jnp.concatenate([choice] * pieces, axis=0)
        square = jnp.zeros((rows, unit), jnp.float32)
        for axis in range(3):
            offset = jnp.dot(
                table[axis * rows:(axis + 1) * rows, :], choice, preferred_element_type=jnp.float32
            )
            square = square + offset * offset
        distance = square * lax.rsqrt(jnp.maximum(square, 1e-30))
        power = jnp.exp2(distance * (log2_e / softness) - cutoff_dist * log2_e / softness)
        contact = (1.0 / (1.0 + power)).astype(jnp.bfloat16)
        contact_ref[:, here] = contact
        total = total + lax.dot_general(
            contact, weights[:, here], (((1,), (1,)), ((), ())), preferred_element_type=jnp.float32
        )
    sums_ref[...] += total

    @pl.when(step == pl.num_programs(0) - 1)
    def finish():
        parts = out_ref.shape[0]
        part, few = rows // parts, latents // parts
        lean = jnp.broadcast_to(jnp.sum(lean_ref[...], axis=1, keepdims=True), (latents, latents))
        small = jnp.concatenate([gram_ref[...], lean], axis=1)
        for i in range(parts):
            out_ref[i, :part] = sums_ref[i * part:(i + 1) * part, :]
            out_ref[i, part:] = small[i * few:(i + 1) * few]


def contacts(coords, first, second, enc_weight, dec_weight, dec_bias):
    rows, _, residues = coords.shape
    latents, pairs = enc_weight.shape
    width = min(512, pairs)
    parts = lax.axis_size("pairs")
    sent = (parts, (rows + latents) // parts, 2 * latents)
    row = pl.BlockSpec((1, width), lambda i: (0, i))
    block = pl.BlockSpec((latents, width), lambda i: (0, i))
    return pl.pallas_call(
        contact_kernel,
        grid=(pairs // width,),
        in_specs=[pl.BlockSpec((3, rows, residues), lambda i: (0, 0, 0)), pl.BlockSpec(memory_space=pltpu.SMEM), row, block, block, row],
        out_specs=[
            pl.BlockSpec((rows, width), lambda i: (0, i)),
            pl.BlockSpec(sent, lambda i: (0, 0, 0)),
        ],
        out_shape=[
            jax.ShapeDtypeStruct((rows, pairs), jnp.bfloat16),
            jax.ShapeDtypeStruct(sent, jnp.float32),
        ],
        scratch_shapes=[
            pltpu.VMEM((3 * rows, pieces * residues), jnp.bfloat16),
            pltpu.VMEM((2 * latents, width), jnp.bfloat16),
            pltpu.VMEM((rows, 2 * latents), jnp.float32),
            pltpu.VMEM((latents, latents), jnp.float32),
            pltpu.VMEM((latents, 128), jnp.float32),
        ],
        compiler_params=pltpu.CompilerParams(vmem_limit_bytes=60 * 2**20),
        cost_estimate=pl.CostEstimate(
            flops=2 * 3 * rows * pieces * residues * pairs,
            bytes_accessed=4 * rows * pairs,
            transcendentals=3 * rows * pairs,
        ),
        name="contacts",
    )(jnp.transpose(coords, (1, 0, 2)), first, second, enc_weight, dec_weight, dec_bias)


def encode(value, latents):
    size, width = value.shape[0], value.shape[-1]
    peaks = [
        jnp.maximum(jnp.max(jnp.max(jnp.abs(rows), axis=0), axis=0, keepdims=True), 1e-30)
        for rows in (value[:, :latents], value[:, latents:])
    ]
    both = lambda low, high, rows: jnp.concatenate(
        [jnp.broadcast_to(low, (rows, width)), jnp.broadcast_to(high, (rows, width))], axis=0
    )
    factor = both(32767.0 / peaks[0], 32767.0 / peaks[1], latents)
    codes = jnp.round(value * factor[None]).astype(jnp.int32).astype(jnp.int16)
    first_rows = lax.broadcasted_iota(jnp.int32, (8, width), 0) < 4
    steps = jnp.where(first_rows, peaks[0] * (1.0 / 32767.0), peaks[1] * (1.0 / 32767.0))
    return codes, steps


def decode(codes, steps, latents):
    width = steps.shape[-1]
    factor = jnp.concatenate(
        [jnp.broadcast_to(steps[:1], (latents, width)), jnp.broadcast_to(steps[4:5], (latents, width))], axis=0
    )
    return codes.astype(jnp.int32).astype(jnp.float32) * factor


def tail_kernel(
    chunks, lag_ref, scale_ref, enc_bias_ref, sums_ref, bias_ref, dec_any, contact_any,
    out_ref, step_ref, contact_ref, dec_ref, zrecv, whole, seen_send, seen_recv, lat_send, lat_recv, left_ref,
    partial_sum, arrived, code_send, step_send, code_recv, step_recv,
    load_sem, z_send, z_recv, side_send, side_recv, half_send, half_recv, full_send, full_recv,
):
    frames, pairs = lax.axis_size("frames"), lax.axis_size("pairs")
    me, depth = lax.axis_index("frames"), lax.axis_index("pairs")
    bits = frames.bit_length() - 1
    rows, latents = contact_any.shape[0], dec_ref.shape[0]
    part = rows // pairs
    width = dec_ref.shape[1] // chunks
    shard = width // frames
    half = rows // 2

    def partner(bit):
        return me + (1 << bit) - 2 * (1 << bit) * (lax.div(me, 1 << bit) % 2)

    def bit_of(bit):
        return lax.div(me, 1 << bit) % 2

    following, previous = lax.rem(me + 1, frames), lax.rem(me + frames - 1, frames)

    loads = [
        pltpu.make_async_copy(dec_any, dec_ref, load_sem.at[0]),
        pltpu.make_async_copy(contact_any, contact_ref, load_sem.at[1]),
    ]
    for copy in loads:
        copy.start()
    barrier = pltpu.get_barrier_semaphore()
    for step in range(1, pairs):
        pl.semaphore_signal(
            barrier, inc=1, device_id={"pairs": lax.rem(depth + step, pairs)}, device_id_type=pl.DeviceIdType.MESH
        )
    for other in [following, previous] + [partner(b) for b in range(bits)]:
        pl.semaphore_signal(barrier, inc=1, device_id={"frames": other}, device_id_type=pl.DeviceIdType.MESH)
    pl.semaphore_wait(barrier, pairs - 1 + 2 + bits)

    scatter = []
    for step in range(1, pairs):
        other = lax.rem(depth + step, pairs)
        copy = pltpu.make_async_remote_copy(
            src_ref=sums_ref.at[other],
            dst_ref=zrecv.at[step - 1],
            send_sem=z_send.at[0, step - 1],
            recv_sem=z_recv.at[0, step - 1],
            device_id={"pairs": other},
            device_id_type=pl.DeviceIdType.MESH,
        )
        copy.start()
        scatter.append(copy)
    total = sums_ref[depth]
    for step in range(1, pairs):
        scatter[step - 1].wait_recv()
        total = total + zrecv[step - 1]
    whole[depth] = total
    gather = []
    for step in range(1, pairs):
        copy = pltpu.make_async_remote_copy(
            src_ref=whole.at[depth],
            dst_ref=whole.at[depth],
            send_sem=z_send.at[1, step - 1],
            recv_sem=z_recv.at[1, step - 1],
            device_id={"pairs": lax.rem(depth + step, pairs)},
            device_id_type=pl.DeviceIdType.MESH,
        )
        copy.start()
        gather.append(copy)
    for copy in gather:
        copy.wait_recv()

    sums = jnp.concatenate([whole[i, :part] for i in range(pairs)], axis=0)
    small = jnp.concatenate([whole[i, part:] for i in range(pairs)], axis=0)
    gram = small[:, :latents]
    lean = jnp.transpose(small)[latents:latents + 1, :]
    latent = jnp.tanh(sums[:, :latents] + enc_bias_ref[...])
    latent_bf = latent.astype(jnp.bfloat16)
    seen = sums[:, latents:]
    seen_send[...] = jnp.concatenate([seen[:half], seen[half:]], axis=1)
    lat_send[...] = jnp.concatenate([latent_bf[:half], latent_bf[half:]], axis=1)
    sides = []
    for i, (source, target, other) in enumerate(
        [(seen_send, seen_recv, previous), (lat_send, lat_recv, following)]
    ):
        copy = pltpu.make_async_remote_copy(
            src_ref=source,
            dst_ref=target,
            send_sem=side_send.at[i],
            recv_sem=side_recv.at[i],
            device_id={"frames": other},
            device_id_type=pl.DeviceIdType.MESH,
        )
        copy.start()
        sides.append(copy)

    lag = lag_ref[...]
    scale = scale_ref[...]
    frame = lax.broadcasted_iota(jnp.int32, (rows, 1), 0)
    usable = me * rows + frame + lag < rows * frames
    used = jnp.where(usable, latent_bf.astype(jnp.float32), 0.0).astype(jnp.bfloat16)
    mix = lax.dot_general(used, used, (((0,), (0,)), ((), ())), preferred_element_type=jnp.float32)
    tilt = lax.dot_general(
        used, jnp.ones((rows, 128), jnp.bfloat16), (((0,), (0,)), ((), ())), preferred_element_type=jnp.float32
    )[:, :1]
    mix_parts = jnp.concatenate(split(mix, 3), axis=1)
    decoded = lean
    for piece in split(gram, 3):
        decoded = decoded + jnp.dot(latent_bf, piece, preferred_element_type=jnp.float32)
    for copy in sides:
        copy.wait_recv()
    seen_all = jnp.concatenate([seen, seen_recv[:, :latents], seen_recv[:, latents:]], axis=0)
    latent_all = jnp.concatenate([lat_recv[:, :latents], lat_recv[:, latents:], latent_bf], axis=0)
    place = lax.broadcasted_iota(jnp.int32, (rows, 2 * rows), 1)
    pick_later = jnp.where(place == frame + lag, 1.0, 0.0).astype(jnp.bfloat16)
    pick_earlier = jnp.where(place == frame + rows - lag, 1.0, 0.0).astype(jnp.bfloat16)
    later = jnp.zeros((rows, latents), jnp.float32)
    for piece in split(seen_all, 3):
        later = later + jnp.dot(pick_later, piece, preferred_element_type=jnp.float32)
    earlier = jnp.dot(pick_earlier, latent_all, preferred_element_type=jnp.float32)
    earlier = jnp.where(me * rows + frame >= lag, earlier, 0.0)
    backward = jnp.where(usable, (decoded - later) * scale, 0.0)
    hidden = backward * (1.0 - latent * latent)
    left_ref[...] = jnp.transpose(jnp.concatenate([hidden, earlier], axis=1)).astype(jnp.bfloat16)
    for copy in loads:
        copy.wait()

    def order(color):
        turn = color % max(bits - 1, 1)
        later_bits = list(range(1, bits))
        return [0] + later_bits[turn:] + later_bits[:turn]

    def begin_of(sequence, count):
        begin = 0
        for k in range(count):
            begin = begin + bit_of(sequence[k]) * (frames >> (k + 1))
        return begin

    def remote(source, target, sender, receiver, bit):
        return pltpu.make_async_remote_copy(
            src_ref=source,
            dst_ref=target,
            send_sem=sender,
            recv_sem=receiver,
            device_id={"frames": partner(bit)},
            device_id_type=pl.DeviceIdType.MESH,
        )

    def halving(chunk, sequence, k):
        size = frames >> (k + 1)
        if k == 0:
            begin = (1 - bit_of(sequence[0])) * size
            return [
                remote(
                    partial_sum.at[chunk, pl.ds(begin, size)], arrived.at[chunk],
                    half_send.at[0, chunk, k], half_recv.at[0, chunk, k], sequence[k],
                )
            ]
        here = pl.ds(frames // 2 - 2 * size, size)
        return [
            remote(
                code_send.at[chunk, here], code_recv.at[chunk, here],
                half_send.at[0, chunk, k], half_recv.at[0, chunk, k], sequence[k],
            ),
            remote(
                step_send.at[chunk, k - 1], step_recv.at[chunk, k - 1],
                half_send.at[1, chunk, k], half_recv.at[1, chunk, k], sequence[k],
            ),
        ]

    def doubling(chunk, sequence, k):
        here = pl.ds(begin_of(sequence, k + 1), frames >> (k + 1))
        return [
            remote(
                ref.at[chunk, here], ref.at[chunk, here],
                full_send.at[i, chunk, k], full_recv.at[i, chunk, k], sequence[k],
            )
            for i, ref in enumerate((out_ref, step_ref))
        ]

    def each_chunk(body):
        def pair(index, carry):
            for color in range(2):
                body(index * 2 + color, order(color))
            return carry

        lax.fori_loop(0, chunks // 2, pair, 0)

    def multiply(chunk, sequence):
        columns = pl.ds(pl.multiple_of(chunk * width, width), width)
        product = jnp.dot(left_ref[...], contact_ref[:, columns], preferred_element_type=jnp.float32)
        dec = dec_ref[:, columns]
        own = jnp.dot(mix_parts, jnp.concatenate([dec, dec, dec], axis=0), preferred_element_type=jnp.float32)
        decode = scale * (own + tilt * bias_ref[:, columns] - product[latents:])
        for i in range(frames):
            here = slice(i * shard, (i + 1) * shard)
            partial_sum[chunk, i, :latents] = product[:latents, here]
            partial_sum[chunk, i, latents:] = decode[:, here]
        for copy in halving(chunk, sequence, 0):
            copy.start()

    each_chunk(multiply)
    for k in range(bits):
        def reduce(chunk, sequence, k=k):
            for copy in halving(chunk, sequence, k):
                copy.wait_recv()
            size = frames >> (k + 1)
            begin = begin_of(sequence, k + 1)
            if k == 0:
                came = arrived[chunk]
            else:
                codes = code_recv[chunk, pl.ds(frames // 2 - 2 * size, size)]
                came = decode(codes, step_recv[chunk, k - 1], latents)
            added = partial_sum[chunk, pl.ds(begin, size)] + came
            if k < bits - 1:
                half_size = size // 2
                turn = bit_of(sequence[k + 1])
                partial_sum[chunk, pl.ds(begin, size)] = added
                leaving = partial_sum[chunk, pl.ds(begin + (1 - turn) * half_size, half_size)]
                codes, steps = encode(leaving, latents)
                code_send[chunk, pl.ds(frames // 2 - 2 * half_size, half_size)] = codes
                step_send[chunk, k] = steps
                for copy in halving(chunk, sequence, k + 1):
                    copy.start()
            else:
                codes, steps = encode(added, latents)
                out_ref[chunk, pl.ds(begin, 1)] = codes
                step_ref[chunk, begin] = steps
                for copy in doubling(chunk, sequence, k):
                    copy.start()

        each_chunk(reduce)
    for k in reversed(range(bits)):
        def spread(chunk, sequence, k=k):
            for copy in doubling(chunk, sequence, k):
                copy.wait_recv()
            if k > 0:
                for copy in doubling(chunk, sequence, k - 1):
                    copy.start()

        each_chunk(spread)

    def finish(chunk, sequence):
        for k in range(bits):
            for copy in halving(chunk, sequence, k) + doubling(chunk, sequence, k):
                copy.wait_send()

    each_chunk(finish)
    for copy in scatter + gather + sides:
        copy.wait_send()


def tail(lag, scale, enc_bias, sums, dec_weight, dec_bias, contact):
    rows, pairs = contact.shape
    latents = dec_weight.shape[0]
    frames, depth = lax.axis_size("frames"), lax.axis_size("pairs")
    bits = frames.bit_length() - 1
    chunks = 2 * max(1, min(4, pairs // (2 * frames * 128)))
    shard = pairs // chunks // frames
    vmem = pl.BlockSpec(memory_space=pltpu.VMEM)
    dma = pltpu.SemaphoreType.DMA
    return pl.pallas_call(
        partial(tail_kernel, chunks),
        in_specs=[vmem] * 5 + [pl.BlockSpec(memory_space=pl.ANY)] * 2,
        out_specs=[vmem, vmem],
        out_shape=[
            jax.ShapeDtypeStruct((chunks, frames, 2 * latents, shard), jnp.int16),
            jax.ShapeDtypeStruct((chunks, frames, 8, shard), jnp.float32),
        ],
        scratch_shapes=[
            pltpu.VMEM((rows, pairs), jnp.bfloat16),
            pltpu.VMEM(dec_weight.shape, jnp.bfloat16),
            pltpu.VMEM((depth - 1, *sums.shape[1:]), jnp.float32),
            pltpu.VMEM(sums.shape, jnp.float32),
            pltpu.VMEM((rows // 2, 2 * latents), jnp.float32),
            pltpu.VMEM((rows // 2, 2 * latents), jnp.float32),
            pltpu.VMEM((rows // 2, 2 * latents), jnp.bfloat16),
            pltpu.VMEM((rows // 2, 2 * latents), jnp.bfloat16),
            pltpu.VMEM((2 * latents, rows), jnp.bfloat16),
            pltpu.VMEM((chunks, frames, 2 * latents, shard), jnp.float32),
            pltpu.VMEM((chunks, frames // 2, 2 * latents, shard), jnp.float32),
            pltpu.VMEM((chunks, max(1, frames // 2 - 1), 2 * latents, shard), jnp.int16),
            pltpu.VMEM((chunks, max(1, bits - 1), 8, shard), jnp.float32),
            pltpu.VMEM((chunks, max(1, frames // 2 - 1), 2 * latents, shard), jnp.int16),
            pltpu.VMEM((chunks, max(1, bits - 1), 8, shard), jnp.float32),
            dma((2,)),
            dma((2, depth - 1)),
            dma((2, depth - 1)),
            dma((2,)),
            dma((2,)),
            dma((2, chunks, bits)),
            dma((2, chunks, bits)),
            dma((2, chunks, bits)),
            dma((2, chunks, bits)),
        ],
        compiler_params=pltpu.CompilerParams(
            vmem_limit_bytes=60 * 2**20, collective_id=0, has_side_effects=True
        ),
        name="tail",
    )(lag, scale, enc_bias, sums, dec_bias, dec_weight, contact)


def decode_kernel(code_any, step_any, enc_out, dec_out, code_ref, step_ref, values, come_sems, sems):
    chunks, frames, rows, shard = code_any.shape
    latents, width = rows // 2, frames * shard

    def leave(chunk):
        here = pl.ds(pl.multiple_of(chunk * width, width), width)
        return [
            pltpu.make_async_copy(values.at[chunk, i], out.at[:, here], sems.at[i, chunk])
            for i, out in enumerate((enc_out, dec_out))
        ]

    def enter(chunk):
        return [
            pltpu.make_async_copy(code_any.at[chunk], code_ref.at[chunk], come_sems.at[0, chunk]),
            pltpu.make_async_copy(step_any.at[chunk], step_ref.at[chunk], come_sems.at[1, chunk]),
        ]

    def begin(chunk, carry):
        for copy in enter(chunk):
            copy.start()
        return carry

    lax.fori_loop(0, chunks, begin, 0)

    def one(chunk, carry):
        for copy in enter(chunk):
            copy.wait()
        for i in range(frames):
            value = decode(code_ref[chunk, i], step_ref[chunk, i], latents)
            values[chunk, 0, :, i * shard:(i + 1) * shard] = value[:latents]
            values[chunk, 1, :, i * shard:(i + 1) * shard] = value[latents:]
        for copy in leave(chunk):
            copy.start()
        return carry

    lax.fori_loop(0, chunks, one, 0)

    def end(chunk, carry):
        for copy in leave(chunk):
            copy.wait()
        return carry

    lax.fori_loop(0, chunks, end, 0)


def decoded_outputs(codes, steps):
    chunks, frames, rows, shard = codes.shape
    latents, width = rows // 2, frames * shard
    return pl.pallas_call(
        decode_kernel,
        in_specs=[pl.BlockSpec(memory_space=pl.ANY)] * 2,
        out_specs=[pl.BlockSpec(memory_space=pl.ANY)] * 2,
        out_shape=[jax.ShapeDtypeStruct((latents, chunks * width), jnp.float32)] * 2,
        scratch_shapes=[
            pltpu.VMEM(codes.shape, codes.dtype),
            pltpu.VMEM(steps.shape, steps.dtype),
            pltpu.VMEM((chunks, 2, latents, width), jnp.float32),
            pltpu.SemaphoreType.DMA((2, chunks)),
            pltpu.SemaphoreType.DMA((2, chunks)),
        ],
        compiler_params=pltpu.CompilerParams(vmem_limit_bytes=60 * 2**20),
        name="decode",
    )(codes, steps)


def local(coords, pair_first, pair_second, enc_weight, enc_bias, dec_weight, dec_bias, lag_frames):
    rows = coords.shape[0]
    latents, pairs = enc_weight.shape
    total_frames = rows * lax.axis_size("frames")
    bias = dec_bias.reshape(1, pairs)
    contact, sums = contacts(coords, pair_first, pair_second.reshape(1, pairs), enc_weight, dec_weight, bias)
    scale = 1.0 / jnp.sqrt(jnp.float32(total_frames) - lag_frames.astype(jnp.float32))
    codes, steps = tail(
        lag_frames.reshape(1, 1), scale.reshape(1, 1), enc_bias.reshape(1, latents), sums,
        dec_weight, bias, contact,
    )
    return tuple(decoded_outputs(codes, steps))


def solution(mesh):
    placed = (
        P("frames", None, None),
        P("pairs"),
        P("pairs"),
        P(None, "pairs"),
        P(),
        P(None, "pairs"),
        P("pairs"),
        P(),
    )
    return jax.shard_map(
        local,
        mesh=mesh,
        in_specs=placed,
        out_specs=(P(None, "pairs"), P(None, "pairs")),
        check_vma=False,
    )
```
